32 devices in a mesh: sec: 4 (over x, core), row: 8 (over z, y).
Axes of the slice: x: 2, y: 2, z: 4, core: 2. Of those that a mesh axis runs over, the one named last changes fastest.
Arguments:
- template_scan: float32 [32, 1024, 256], P('sec', 'row'), may hold values from -6 to 6
- reference_scan: float32 [32, 1024, 256], P('sec', 'row'), may hold values from -6 to 6
- velocity: float32 [3, 32, 256, 1024], P(None, 'sec', 'row'), may hold values from -0.75 to 0.75
- stiffness: float32 [32, 256, 1024], P('sec', 'row'), may hold values from 0.02 to 0.2
Outputs:
- gradient: float32 [3, 32, 256, 1024], P(None, 'sec', 'row')
- objective: float32 [], replicated
The draws below stay inside these ranges and needn't reach their ends.
All inputs are finite; a program needn't handle non-finite values.
Results may differ from the reference program's by a relative error of at most 0.00002.
Values sent between devices are 32-bit elements; how exact they have to be, the bound alone decides.
No kernel may reach another device: no remote copies, remote signals or barrier semaphores. Data moves between devices by JAX's collectives and lax.ppermute only.
A program may use at most 128 MiB of HBM per device.

```python
import math
import jax
import jax.numpy as jnp

NY = 1024
STEPS = 4
NZ = 32
NX = 256


def block_scale(stream_key, shape, split, low, top_value):
    def one(axis_at, shards_of):
        heights = jax.random.uniform(jax.random.fold_in(jax.random.fold_in(stream_key, 6), axis_at), (shards_of,), jnp.float32, low / len(split), top_value / len(split))
        return jnp.repeat(jnp.exp(heights), shape[axis_at] // shards_of).reshape((-1,) + (1,) * (len(shape) - axis_at - 1))

    gain = one(*split[0])
    for cut in split[1:]:
        gain = gain * one(*cut)
    return gain


def scatter_about(key, shape, width, limit, shards=(), kind=jnp.bfloat16):
    drawn = jax.random.normal(key, shape, jnp.float32) * width
    if len(shards) > 0:
        drawn = block_scale(key, shape, shards, -0.22, 0.18) * drawn
    return jnp.clip(drawn, min=-limit, max=limit).astype(kind)


def setup_inputs(seed: int = 0) -> dict:
    key_of = jax.random.split(jax.random.key(seed), 5)
    return {
        "template_scan": scatter_about(key_of[0], (NZ, NY, NX), 1.0, 6.0, ((0, 4), (1, 8)), jnp.float32),
        "reference_scan": scatter_about(key_of[1], (NZ, NY, NX), 1.0, 6.0, ((0, 4), (1, 8)), jnp.float32),
        "velocity": scatter_about(key_of[2], (3, NZ, NX, NY), 0.3, 0.75, ((1, 4), (2, 8)), jnp.float32),
        "stiffness": jnp.clip(jnp.exp(math.log(0.2) - 2.3025851 * jax.random.uniform(key_of[3], (NZ, NX, NY), jnp.float32) ** block_scale(key_of[3], (NZ, NX, NY), ((0, 4), (1, 8)), -0.2, 0.2)), 0.02, 0.2),
    }


DT = 0.25
KAPPA = 0.5
BETA = 0.5


def shifted(padded, direction, offset):
    cuts = [slice(1, -1), slice(1, -1), slice(1, -1)]
    cuts[direction] = slice(1 + offset, padded.shape[direction] - 1 + offset)
    return padded[tuple(cuts)]


def middle(padded):
    return padded[1:-1, 1:-1, 1:-1]


def centred(padded, direction):
    return (shifted(padded, direction, 1) - shifted(padded, direction, -1)) * 0.5


def laplace(padded):
    summed = shifted(padded, 0, 1) + shifted(padded, 0, -1)
    summed = summed + shifted(padded, 1, 1) + shifted(padded, 1, -1)
    summed = summed + shifted(padded, 2, 1) + shifted(padded, 2, -1)
    return summed - 6.0 * middle(padded)


def forward_step(padded, velocity):
    advect = velocity[0] * centred(padded, 0) + velocity[1] * centred(padded, 1) + velocity[2] * centred(padded, 2)
    return middle(padded) - DT * advect + DT * KAPPA * laplace(padded)


def adjoint_step(pad_adj, pad_prod):
    spread = centred(pad_prod[0], 0) + centred(pad_prod[1], 1) + centred(pad_prod[2], 2)
    return middle(pad_adj) + DT * spread + DT * KAPPA * laplace(pad_adj)


def regular(pad_vel, pad_stiff):
    s_mid = middle(pad_stiff)
    results = []
    for component in range(3):
        v_mid = middle(pad_vel[component])
        accum = jnp.zeros_like(v_mid)
        for direction in range(3):
            face_low = 0.5 * (s_mid + shifted(pad_stiff, direction, -1))
            face_high = 0.5 * (s_mid + shifted(pad_stiff, direction, 1))
            accum = accum + face_low * (v_mid - shifted(pad_vel[component], direction, -1)) - face_high * (shifted(pad_vel[component], direction, 1) - v_mid)
        results.append(accum)
    return jnp.stack(results)


def reference(template_scan, reference_scan, velocity, stiffness):
    template = jnp.swapaxes(template_scan, 1, 2)
    fixed = jnp.swapaxes(reference_scan, 1, 2)
    pad_vel = jnp.pad(velocity, ((0, 0), (1, 1), (1, 1), (1, 1)))
    pad_stiff = jnp.pad(stiffness, 1)
    moved = template
    stored = []
    for step_index in range(STEPS):
        padded = jnp.pad(moved, 1)
        stored.append(padded)
        moved = forward_step(padded, velocity)
    misfit = moved - fixed
    data_sum = jnp.sum(misfit * misfit)
    adjoint = misfit
    data_grad = jnp.zeros(velocity.shape, jnp.float32)
    for step_index in range(STEPS - 1, -1, -1):
        padded = stored[step_index]
        slopes = jnp.stack([centred(padded, 0), centred(padded, 1), centred(padded, 2)])
        data_grad = data_grad - DT * adjoint[None] * slopes
        if step_index > 0:
            pad_adj = jnp.pad(adjoint, 1)
            pad_prod = jnp.pad(velocity * adjoint[None], ((0, 0), (1, 1), (1, 1), (1, 1)))
            adjoint = adjoint_step(pad_adj, pad_prod)
    stiff_term = regular(pad_vel, pad_stiff)
    reg_sum = jnp.sum(velocity * stiff_term)
    gradient = BETA * stiff_term + data_grad
    objective = (0.5 * data_sum + 0.5 * BETA * reg_sum) / (NZ * NX * NY)
    return gradient, objective
```

```python
import jax
import jax.numpy as jnp
from jax import lax
from jax.experimental import pallas as pl
from jax.experimental.pallas import tpu as pltpu
from jax.sharding import PartitionSpec as P

STEPS = 4

DT = 0.25
KAPPA = 0.5
BETA = 0.5

LANES = 128
TILE = 8
GAP = 8
SENT = 4
WIDE = STEPS - 1
WEIGHT = DT * KAPPA
SELF = 1.0 - 6.0 * WEIGHT
assert WEIGHT == DT * 0.5

VMEM = pl.BlockSpec(memory_space=pltpu.VMEM)
SMEM = pl.BlockSpec(memory_space=pltpu.SMEM)
ANY = pl.BlockSpec(memory_space=pl.ANY)


def exchange(low_part, high_part, axis):
    count = lax.axis_size(axis)
    below = lax.ppermute(high_part, axis, [(i, i + 1) for i in range(count - 1)])
    above = lax.ppermute(low_part, axis, [(i + 1, i) for i in range(count - 1)])
    return below, above


def columns(tiles):
    lane = lax.broadcasted_iota(jnp.int32, tiles[0].shape, 1)
    zero = jnp.zeros_like(tiles[0])
    up = [pltpu.roll(t, LANES - 1, 1) for t in tiles]
    down = [pltpu.roll(t, 1, 1) for t in tiles]
    plus = [jnp.where(lane == LANES - 1, n, u) for u, n in zip(up, up[1:] + [zero])]
    minus = [jnp.where(lane == 0, p, d) for d, p in zip(down, [zero] + down[:-1])]
    return plus, minus


def edges(tiles_up, tiles_down):
    lane = lax.broadcasted_iota(jnp.int32, tiles_up[0].shape, 1)
    zero = jnp.zeros_like(tiles_up[0])
    up = [pltpu.roll(t, LANES - 1, 1) for t in tiles_up]
    down = [pltpu.roll(t, 1, 1) for t in tiles_down]
    plus = [jnp.where(lane == LANES - 1, n, u) for u, n in zip(up, up[1:] + [zero])]
    minus = [jnp.where(lane == 0, p, d) for d, p in zip(down, [zero] + down[:-1])]
    return plus, minus


def fill(out, own, below, above, before, after, width):
    blocks, sections, rows, _ = own.shape

    def plane(src, z_src, z_out):
        for i in range(blocks):
            out[i, z_out, pl.ds(GAP, rows), :] = src[i, z_src, :, :]

    def whole(z, _):
        plane(own, z, z + width)
        return 0

    def halo(z, _):
        plane(below, z, z)
        plane(above, z, z + width + sections)
        return 0

    def sides(z, _):
        for i in range(blocks):
            out[i, z, pl.ds(GAP - SENT, SENT), :] = before[i, z, :, :]
            out[i, z, pl.ds(GAP + rows, SENT), :] = after[i, z, :, :]
        return 0

    lax.fori_loop(0, sections, whole, 0)
    lax.fori_loop(0, width, halo, 0)
    lax.fori_loop(0, sections + 2 * width, sides, 0)


def groups(rows, reach):
    if reach == 0:
        return [GAP + g for g in range(0, rows, TILE)]
    return [GAP - SENT + g for g in range(0, rows + TILE, TILE)]


def masked(value, start, rows, flags):
    row = start + lax.broadcasted_iota(jnp.int32, value.shape, 0)
    if start < GAP:
        return jnp.where((row >= GAP) | (flags[2] > 0.5), value, 0.0)
    if start + TILE > GAP + rows:
        return jnp.where((row < GAP + rows) | (flags[3] > 0.5), value, 0.0)
    return value


def weights(flags, z, low, high):
    factor = jnp.where(z < low, flags[0], jnp.where(z >= high, flags[1], 1.0))
    return SELF * factor, WEIGHT * factor


def forward_kernel(flags, own, below, above, before, after, vel, moved_ref, kept_ref, *scratch):
    levels, sem = scratch[:STEPS], scratch[STEPS]
    blocks, sections, rows, _ = own.shape
    fill(levels[0], own, below, above, before, after, STEPS)
    copies = []
    for step in range(STEPS):
        src = levels[step]
        copies.append(
            pltpu.make_async_copy(
                src.at[:, pl.ds(STEPS - 1, sections + 2), :, :], kept_ref.at[step], sem.at[step]
            )
        )
        copies[-1].start()
        reach = STEPS - 1 - step

        def plane(z, _, src=src, step=step, reach=reach):
            keep, weight = weights(flags, z, STEPS, STEPS + sections)
            for r in groups(rows, reach):
                here = pl.ds(r, TILE)
                mids = [src[i, z, here, :] for i in range(blocks)]
                plus, minus = columns(mids)
                for i in range(blocks):
                    zp, zm = src[i, z + 1, here, :], src[i, z - 1, here, :]
                    xp, xm = src[i, z, pl.ds(r + 1, TILE), :], src[i, z, pl.ds(r - 1, TILE), :]
                    yp, ym = plus[i], minus[i]
                    total = (zp + zm) - vel[0, i, z - 1, here, :] * (zp - zm)
                    total = total + ((xp + xm) - vel[1, i, z - 1, here, :] * (xp - xm))
                    total = total + ((yp + ym) - vel[2, i, z - 1, here, :] * (yp - ym))
                    value = keep * mids[i] + weight * total
                    if step == STEPS - 1:
                        moved_ref[i, z - STEPS, pl.ds(r - GAP, TILE), :] = value
                    else:
                        levels[step + 1][i, z, here, :] = masked(value, r, rows, flags)
            return 0

        lax.fori_loop(STEPS - reach, STEPS + sections + reach, plane, 0)
    for copy in copies:
        copy.wait()


def adjoint_kernel(flags, own, below, above, before, after, vel, kept, reg, grad_ref, *levels):
    blocks, sections, rows, _ = own.shape
    fill(levels[0], own, below, above, before, after, WIDE)
    for step in range(WIDE):
        src, out = levels[step], levels[step + 1]
        reach = WIDE - 1 - step

        def plane(z, _, src=src, out=out, reach=reach):
            keep, weight = weights(flags, z, WIDE, WIDE + sections)
            for r in groups(rows, reach):
                here, up, down = pl.ds(r, TILE), pl.ds(r + 1, TILE), pl.ds(r - 1, TILE)
                mids = [src[i, z, here, :] for i in range(blocks)]
                prods = [mids[i] * vel[2, i, z, here, :] for i in range(blocks)]
                plus, minus = edges(
                    [m + p for m, p in zip(mids, prods)], [m - p for m, p in zip(mids, prods)]
                )
                for i in range(blocks):
                    zp, zm = src[i, z + 1, here, :], src[i, z - 1, here, :]
                    xp, xm = src[i, z, up, :], src[i, z, down, :]
                    total = plus[i] + minus[i]
                    total = total + (zp + zp * vel[0, i, z + 1, here, :])
                    total = total + (zm - zm * vel[0, i, z - 1, here, :])
                    total = total + (xp + xp * vel[1, i, z, up, :])
                    total = total + (xm - xm * vel[1, i, z, down, :])
                    value = keep * mids[i] + weight * total
                    if reach > 0:
                        value = masked(value, r, rows, flags)
                    out[i, z, here, :] = value
            return 0

        lax.fori_loop(WIDE - reach, WIDE + sections + reach, plane, 0)

    def slope(z, _):
        for r in groups(rows, 0):
            here, up, down = pl.ds(r, TILE), pl.ds(r + 1, TILE), pl.ds(r - 1, TILE)
            at = pl.ds(r - GAP, TILE)
            sums = [[None] * 3 for _ in range(blocks)]
            for k in range(STEPS):
                adj = [levels[STEPS - 1 - k][i, z + WIDE, here, :] for i in range(blocks)]
                plus, minus = columns([kept[k, i, z + 1, here, :] for i in range(blocks)])
                for i in range(blocks):
                    parts = (
                        adj[i] * (kept[k, i, z + 2, here, :] - kept[k, i, z, here, :]),
                        adj[i] * (kept[k, i, z + 1, up, :] - kept[k, i, z + 1, down, :]),
                        adj[i] * (plus[i] - minus[i]),
                    )
                    for a in range(3):
                        sums[i][a] = parts[a] if k == 0 else sums[i][a] + parts[a]
            for i in range(blocks):
                lanes = pl.ds(i * LANES, LANES)
                for a in range(3):
                    grad_ref[a, z, at, lanes] = reg[a, z, at, lanes] - (0.5 * DT) * sums[i][a]
        return 0

    lax.fori_loop(0, sections, slope, 0)


def regular_kernel(vel, vel_below, vel_above, vel_before, vel_after,
                   sti, sti_below, sti_above, sti_before, sti_after,
                   ext_ref, reg_ref, sum_ref, sti_ext):
    _, sections, rows, width = vel.shape
    blocks = width // LANES

    def lay(out, src, z_out, z_src):
        for i in range(blocks):
            out[i, z_out, pl.ds(GAP, rows), :] = src[z_src, :, pl.ds(i * LANES, LANES)]

    def lay_sides(out, z, low, high, count):
        for i in range(blocks):
            lanes = pl.ds(i * LANES, LANES)
            out[i, z, pl.ds(GAP - count, count), :] = low[:, lanes]
            out[i, z, pl.ds(GAP + rows, count), :] = high[:, lanes]

    for c in range(3):
        def mid(z, _, c=c):
            lay(ext_ref.at[c], vel.at[c], z + WIDE, z)
            return 0

        def far(z, _, c=c):
            lay(ext_ref.at[c], vel_below.at[c], z, z)
            lay(ext_ref.at[c], vel_above.at[c], z + WIDE + sections, z)
            return 0

        def side(z, _, c=c):
            lay_sides(ext_ref.at[c], z, vel_before.at[c, z], vel_after.at[c, z], SENT)
            return 0

        lax.fori_loop(0, sections, mid, 0)
        lax.fori_loop(0, WIDE, far, 0)
        lax.fori_loop(0, sections + 2 * WIDE, side, 0)

    lay(sti_ext, sti_below, 0, 0)
    lay(sti_ext, sti_above, sections + 1, 0)

    def mid_s(z, _):
        lay(sti_ext, sti, z + 1, z)
        lay_sides(sti_ext, z + 1, sti_before.at[z], sti_after.at[z], 1)
        return 0

    lax.fori_loop(0, sections, mid_s, 0)

    def plane(z, acc):
        for r in groups(rows, 0):
            here, up, down = pl.ds(r, TILE), pl.ds(r + 1, TILE), pl.ds(r - 1, TILE)
            at = pl.ds(r - GAP, TILE)
            s_mid = [sti_ext[i, z + 1, here, :] for i in range(blocks)]
            s_plus, s_minus = columns(s_mid)
            faces = []
            for i in range(blocks):
                s = s_mid[i]
                faces.append([
                    (s + sti_ext[i, z, here, :], s + sti_ext[i, z + 2, here, :]),
                    (s + sti_ext[i, z + 1, down, :], s + sti_ext[i, z + 1, up, :]),
                    (s + s_minus[i], s + s_plus[i]),
                ])
            for c in range(3):
                v_mid = [ext_ref[c, i, z + WIDE, here, :] for i in range(blocks)]
                v_plus, v_minus = columns(v_mid)
                for i in range(blocks):
                    v = v_mid[i]
                    pairs = (
                        (ext_ref[c, i, z + WIDE - 1, here, :], ext_ref[c, i, z + WIDE + 1, here, :]),
                        (ext_ref[c, i, z + WIDE, down, :], ext_ref[c, i, z + WIDE, up, :]),
                        (v_minus[i], v_plus[i]),
                    )
                    total = None
                    for (low, high), (f_low, f_high) in zip(pairs, faces[i]):
                        part = f_low * (v - low) + f_high * (v - high)
                        total = part if total is None else total + part
                    term = (0.5 * BETA) * total
                    reg_ref[c, z, at, pl.ds(i * LANES, LANES)] = term
                    acc = acc + v * term
        return acc

    acc = lax.fori_loop(0, sections, plane, jnp.zeros((TILE, LANES), jnp.float32))
    sum_ref[...] = acc


def to_rows(scan):
    count = lax.axis_size("row")
    sections, width, rows = scan.shape
    own = rows // count
    parts = jnp.swapaxes(scan, 1, 2).reshape(sections, count, own, width).transpose(1, 0, 2, 3)
    parts = lax.all_to_all(parts, "row", split_axis=0, concat_axis=0, tiled=True)
    if width == LANES:
        return parts
    whole = parts.transpose(1, 2, 0, 3).reshape(sections, own, count * width // LANES, LANES)
    return whole.transpose(2, 0, 1, 3)


def with_halos(field, width):
    rows = field.shape[2]
    below, above = exchange(field[:, :width], field[:, -width:], "sec")
    low, high = (
        jnp.concatenate([part[:, :, cut] for part in (below, field, above)], axis=1)
        for cut in (slice(0, SENT), slice(rows - SENT, rows))
    )
    before, after = exchange(low, high, "row")
    return below, above, before, after


def call(kernel, shapes, ins, scratch, megabytes, flops=0):
    return pl.pallas_call(
        kernel,
        out_shape=[jax.ShapeDtypeStruct(shape, jnp.float32) for shape, _ in shapes],
        in_specs=ins,
        out_specs=[spec for _, spec in shapes],
        scratch_shapes=scratch,
        compiler_params=pltpu.CompilerParams(vmem_limit_bytes=megabytes << 20),
        cost_estimate=pl.CostEstimate(flops=flops, bytes_accessed=16 << 20, transcendentals=0),
    )


def local(template_scan, reference_scan, velocity, stiffness):
    _, sections, rows, width = velocity.shape
    blocks = width // LANES
    tall = rows + 2 * GAP
    sec, row = lax.axis_index("sec"), lax.axis_index("row")
    flags = jnp.stack([
        sec > 0, sec < lax.axis_size("sec") - 1, row > 0, row < lax.axis_size("row") - 1
    ]).astype(jnp.float32)

    template = to_rows(template_scan)

    low = jnp.concatenate([velocity[:, :WIDE].reshape(3 * WIDE, rows, width), stiffness[:1]])
    high = jnp.concatenate([velocity[:, -WIDE:].reshape(3 * WIDE, rows, width), stiffness[-1:]])
    below, above = exchange(low, high, "sec")
    vel_below, vel_above = (
        part[:-1].reshape(3, WIDE, rows, width) for part in (below, above)
    )
    sides = []
    for cut in (slice(0, SENT), slice(rows - SENT, rows)):
        vel_cut = jnp.concatenate(
            [vel_below[:, :, cut], velocity[:, :, cut], vel_above[:, :, cut]], axis=1
        )
        sides.append(
            jnp.concatenate([vel_cut.reshape(-1, SENT, width), stiffness[:, cut]], axis=0)
        )
    before, after = exchange(sides[0], sides[1], "row")
    deep = sections + 2 * WIDE
    vel_before, vel_after = (
        part[: 3 * deep].reshape(3, deep, SENT, width) for part in (before, after)
    )
    sti_before = before[3 * deep :, SENT - 1 :]
    sti_after = after[3 * deep :, :1]

    def regular(*args):
        return call(
            regular_kernel,
            [
                ((3, blocks, deep, tall, LANES), VMEM),
                ((3, sections, rows, width), VMEM),
                ((TILE, LANES), VMEM),
            ],
            [VMEM] * 10,
            [pltpu.VMEM((blocks, sections + 2, tall, LANES), jnp.float32)],
            56,
            20 << 20,
        )(*args)

    extended, reg, reg_sums = regular(
        velocity, vel_below, vel_above, vel_before, vel_after,
        stiffness, below[-1:], above[-1:], sti_before, sti_after,
    )

    halos = with_halos(template, STEPS)
    field = (blocks, sections + 2 * STEPS, tall, LANES)
    moved, kept = call(
        forward_kernel,
        [
            ((blocks, sections, rows, LANES), VMEM),
            ((STEPS, blocks, sections + 2, tall, LANES), ANY),
        ],
        [SMEM] + [VMEM] * 6,
        [pltpu.VMEM(field, jnp.float32)] * STEPS + [pltpu.SemaphoreType.DMA((STEPS,))],
        56,
        20 << 20,
    )(flags, template, *halos, extended)

    fixed = to_rows(reference_scan)
    misfit = moved - fixed
    partial = 0.5 * jnp.sum(misfit * misfit) + 0.5 * jnp.sum(reg_sums)
    everyone = lax.axis_size("sec") * lax.axis_size("row")
    spread = lax.all_to_all(
        jnp.full((everyone, LANES), partial), ("sec", "row"), split_axis=0, concat_axis=0, tiled=True
    )
    voxels = sections * rows * width * everyone
    objective = jnp.sum(spread[:, 0]) / voxels

    halos = with_halos(misfit, WIDE)
    (gradient,) = call(
        adjoint_kernel,
        [((3, sections, rows, width), VMEM)],
        [SMEM] + [VMEM] * 8,
        [pltpu.VMEM((blocks, deep, tall, LANES), jnp.float32)] * STEPS,
        56,
        20 << 20,
    )(flags, misfit, *halos, extended, kept, reg)
    return (gradient, objective)


def solution(mesh):
    return jax.shard_map(
        local,
        mesh=mesh,
        in_specs=(
            P("sec", "row", None),
            P("sec", "row", None),
            P(None, "sec", "row", None),
            P("sec", "row", None),
        ),
        out_specs=(P(None, "sec", "row", None), P()),
        check_vma=False,
    )
```

```python
import jax
import jax.numpy as jnp
from jax import lax
from jax.experimental import pallas as pl
from jax.experimental.pallas import tpu as pltpu
from jax.sharding import PartitionSpec as P

STEPS = 4

DT = 0.25
KAPPA = 0.5
BETA = 0.5

LANES = 128
TILE = 8
GAP = 8
SENT = 4
WIDE = STEPS - 1
WEIGHT = DT * KAPPA
SELF = 1.0 - 6.0 * WEIGHT
assert WEIGHT == DT * 0.5

VMEM = pl.BlockSpec(memory_space=pltpu.VMEM)
SMEM = pl.BlockSpec(memory_space=pltpu.SMEM)
ANY = pl.BlockSpec(memory_space=pl.ANY)


def exchange(low_part, high_part, axis):
    count = lax.axis_size(axis)
    below = lax.ppermute(high_part, axis, [(i, i + 1) for i in range(count - 1)])
    above = lax.ppermute(low_part, axis, [(i + 1, i) for i in range(count - 1)])
    return below, above


def edges(tiles_up, tiles_down):
    lane = lax.broadcasted_iota(jnp.int32, tiles_up[0].shape, 1)
    zero = jnp.zeros_like(tiles_up[0])
    up = [pltpu.roll(t, LANES - 1, 1) for t in tiles_up]
    down = [pltpu.roll(t, 1, 1) for t in tiles_down]
    plus = [jnp.where(lane == LANES - 1, n, u) for u, n in zip(up, up[1:] + [zero])]
    minus = [jnp.where(lane == 0, p, d) for d, p in zip(down, [zero] + down[:-1])]
    return plus, minus


def edges_of(tiles):
    return edges(tiles, tiles)


def fill(out, own, below, above, before, after, corners_below, corners_above, width):
    blocks, sections, rows, _ = own.shape
    top, bottom = pl.ds(GAP - SENT, SENT), pl.ds(GAP + rows, SENT)

    def whole(z, _):
        for i in range(blocks):
            out[i, z + width, pl.ds(GAP, rows), :] = own[i, z, :, :]
            out[i, z + width, top, :] = before[i, z, :, :]
            out[i, z + width, bottom, :] = after[i, z, :, :]
        return 0

    def halo(z, _):
        for planes, corners, at in ((below, corners_below, z), (above, corners_above, z + width + sections)):
            for i in range(blocks):
                out[i, at, pl.ds(GAP, rows), :] = planes[i, z, :, :]
                out[i, at, top, :] = corners[i, z, pl.ds(0, SENT), :]
                out[i, at, bottom, :] = corners[i, z, pl.ds(SENT, SENT), :]
        return 0

    lax.fori_loop(0, sections, whole, 0)
    lax.fori_loop(0, width, halo, 0)


def block_kernel(scan, out):
    sections, width, rows = scan.shape
    own = out.shape[2]

    def section(z, _):
        for cut in range(0, rows, width):
            turned = scan[z, :, pl.ds(cut, width)].T
            for r in range(0, width, own):
                out[(cut + r) // own, z, :, :] = turned[r : r + own]
        return 0

    lax.fori_loop(0, sections, section, 0)


def part_kernel(field, low_rows, high_rows, low, high):
    blocks, sections, rows, _ = field.shape
    width = low.shape[1]

    def row_ends(z, _):
        for i in range(blocks):
            low_rows[i, z, :, :] = field[i, z, pl.ds(0, SENT), :]
            high_rows[i, z, :, :] = field[i, z, pl.ds(rows - SENT, SENT), :]
        return 0

    def planes(z, _):
        for i in range(blocks):
            low[i, z, :, :] = field[i, z, :, :]
            high[i, z, :, :] = field[i, z + sections - width, :, :]
        return 0

    lax.fori_loop(0, sections, row_ends, 0)
    lax.fori_loop(0, width, planes, 0)


def misfit_kernel(moved, fixed, sums, misfit, low_rows, high_rows, low, high, total_ref):
    blocks, sections, rows, _ = moved.shape

    def section(z, acc):
        for i in range(blocks):
            for r in range(0, rows, TILE):
                value = moved[i, z, pl.ds(r, TILE), :] - fixed[i, z, pl.ds(r, TILE), :]
                misfit[i, z, pl.ds(r, TILE), :] = value
                acc = acc + value * value
        return acc

    zero = jnp.zeros((TILE, LANES), jnp.float32)
    total_ref[...] = 0.5 * (lax.fori_loop(0, sections, section, zero) + sums[...])
    part_kernel(misfit, low_rows, high_rows, low, high)


def groups(rows, reach):
    if reach == 0:
        return [GAP + g for g in range(0, rows, TILE)]
    return [GAP - SENT + g for g in range(0, rows + TILE, TILE)]


def masked(value, start, rows, flags):
    row = start + lax.broadcasted_iota(jnp.int32, value.shape, 0)
    if start < GAP:
        return jnp.where((row >= GAP) | (flags[2] > 0.5), value, 0.0)
    if start + TILE > GAP + rows:
        return jnp.where((row < GAP + rows) | (flags[3] > 0.5), value, 0.0)
    return value


def weights(flags, z, low, high):
    factor = jnp.where(z < low, flags[0], jnp.where(z >= high, flags[1], 1.0))
    return SELF * factor, WEIGHT * factor


def forward_kernel(flags, own, below, above, before, after, low_corners, high_corners, vel, moved_ref, *levels):
    blocks, sections, rows, _ = own.shape
    fill(levels[0], own, below, above, before, after, low_corners, high_corners, STEPS)
    for step in range(STEPS):
        src = levels[step]
        reach = STEPS - 1 - step

        def plane(z, _, src=src, step=step, reach=reach):
            keep, weight = weights(flags, z, STEPS, STEPS + sections)
            for r in groups(rows, reach):
                here = pl.ds(r, TILE)
                mids = [src[i, z, here, :] for i in range(blocks)]
                plus, minus = edges_of(mids)
                for i in range(blocks):
                    zp, zm = src[i, z + 1, here, :], src[i, z - 1, here, :]
                    xp, xm = src[i, z, pl.ds(r + 1, TILE), :], src[i, z, pl.ds(r - 1, TILE), :]
                    yp, ym = plus[i], minus[i]
                    total = (zp + zm) - vel[0, i, z - 1, here, :] * (zp - zm)
                    total = total + ((xp + xm) - vel[1, i, z - 1, here, :] * (xp - xm))
                    total = total + ((yp + ym) - vel[2, i, z - 1, here, :] * (yp - ym))
                    value = keep * mids[i] + weight * total
                    if step == STEPS - 1:
                        moved_ref[i, z - STEPS, pl.ds(r - GAP, TILE), :] = value
                    else:
                        levels[step + 1][i, z, here, :] = masked(value, r, rows, flags)
            return 0

        lax.fori_loop(STEPS - reach, STEPS + sections + reach, plane, 0)


def adjoint_kernel(flags, own, below, above, before, after, low_corners, high_corners, vel, *refs):
    kept, reg, grad_ref, levels = refs[:STEPS], refs[STEPS], refs[STEPS + 1], refs[STEPS + 2 :]
    blocks, sections, rows, _ = own.shape
    fill(levels[0], own, below, above, before, after, low_corners, high_corners, WIDE)
    for step in range(WIDE):
        src, out = levels[step], levels[step + 1]
        reach = WIDE - 1 - step

        def plane(z, _, src=src, out=out, reach=reach):
            keep, weight = weights(flags, z, WIDE, WIDE + sections)
            for r in groups(rows, reach):
                here, up, down = pl.ds(r, TILE), pl.ds(r + 1, TILE), pl.ds(r - 1, TILE)
                mids = [src[i, z, here, :] for i in range(blocks)]
                prods = [mids[i] * vel[2, i, z, here, :] for i in range(blocks)]
                plus, minus = edges(
                    [m + p for m, p in zip(mids, prods)], [m - p for m, p in zip(mids, prods)]
                )
                for i in range(blocks):
                    zp, zm = src[i, z + 1, here, :], src[i, z - 1, here, :]
                    xp, xm = src[i, z, up, :], src[i, z, down, :]
                    total = plus[i] + minus[i]
                    total = total + (zp + zp * vel[0, i, z + 1, here, :])
                    total = total + (zm - zm * vel[0, i, z - 1, here, :])
                    total = total + (xp + xp * vel[1, i, z, up, :])
                    total = total + (xm - xm * vel[1, i, z, down, :])
                    value = keep * mids[i] + weight * total
                    if reach > 0:
                        value = masked(value, r, rows, flags)
                    out[i, z, here, :] = value
            return 0

        lax.fori_loop(WIDE - reach, WIDE + sections + reach, plane, 0)

    def slope(z, _):
        for r in groups(rows, 0):
            here, up, down = pl.ds(r, TILE), pl.ds(r + 1, TILE), pl.ds(r - 1, TILE)
            at = pl.ds(r - GAP, TILE)
            sums = [[None] * 3 for _ in range(blocks)]
            for k in range(STEPS):
                adj = [levels[STEPS - 1 - k][i, z + WIDE, here, :] for i in range(blocks)]
                plus, minus = edges_of([kept[k][i, z + STEPS, here, :] for i in range(blocks)])
                for i in range(blocks):
                    parts = (
                        adj[i] * (kept[k][i, z + STEPS + 1, here, :] - kept[k][i, z + STEPS - 1, here, :]),
                        adj[i] * (kept[k][i, z + STEPS, up, :] - kept[k][i, z + STEPS, down, :]),
                        adj[i] * (plus[i] - minus[i]),
                    )
                    for a in range(3):
                        sums[i][a] = parts[a] if k == 0 else sums[i][a] + parts[a]
            for i in range(blocks):
                lanes = pl.ds(i * LANES, LANES)
                for a in range(3):
                    grad_ref[a, z, at, lanes] = reg[a, z, at, lanes] - (0.5 * DT) * sums[i][a]
        return 0

    lax.fori_loop(0, sections, slope, 0)


def regular_kernel(vel, sti, planes_below, planes_above, before, after, corners_below, corners_above,
                   ext_ref, reg_ref, sum_ref, sti_ext):
    _, sections, rows, width = vel.shape
    blocks = width // LANES

    def lay(out, src, z):
        for i in range(blocks):
            out[i, z, pl.ds(GAP, rows), :] = src[:, pl.ds(i * LANES, LANES)]

    def lay_rows(out, z, row, src, at, count):
        for i in range(blocks):
            out[i, z, pl.ds(row, count), :] = src[pl.ds(at, count), pl.ds(i * LANES, LANES)]

    def mid(z, _):
        for c in range(3):
            lay(ext_ref.at[c], vel.at[c, z], z + WIDE)
        lay(sti_ext, sti.at[z], z + 1)
        return 0

    def far(z, _):
        for c in range(3):
            lay(ext_ref.at[c], planes_below.at[c * WIDE + z], z)
            lay(ext_ref.at[c], planes_above.at[c * WIDE + z], z + WIDE + sections)
        return 0

    lax.fori_loop(0, sections, mid, 0)
    lax.fori_loop(0, WIDE, far, 0)
    lay(sti_ext, planes_below.at[3 * WIDE], 0)
    lay(sti_ext, planes_above.at[3 * WIDE], sections + 1)
    low, high = GAP - WIDE, GAP + rows
    for c in range(3):
        for z in range(sections):
            at = (c * sections + z) * WIDE
            lay_rows(ext_ref.at[c], z + WIDE, low, before, at, WIDE)
            lay_rows(ext_ref.at[c], z + WIDE, high, after, at, WIDE)
        for z in range(WIDE):
            at, half = (c * WIDE + z) * WIDE, 3 * WIDE * WIDE
            for src, z_out in ((corners_below, z), (corners_above, z + WIDE + sections)):
                lay_rows(ext_ref.at[c], z_out, low, src, at, WIDE)
                lay_rows(ext_ref.at[c], z_out, high, src, at + half, WIDE)
    for z in range(sections):
        at = 3 * sections * WIDE + z
        lay_rows(sti_ext, z + 1, GAP - 1, before, at, 1)
        lay_rows(sti_ext, z + 1, GAP + rows, after, at, 1)

    def plane(z, acc):
        for r in groups(rows, 0):
            here, up, down = pl.ds(r, TILE), pl.ds(r + 1, TILE), pl.ds(r - 1, TILE)
            at = pl.ds(r - GAP, TILE)
            s_mid = [sti_ext[i, z + 1, here, :] for i in range(blocks)]
            s_plus, s_minus = edges_of(s_mid)
            faces = []
            for i in range(blocks):
                s = s_mid[i]
                faces.append([
                    (s + sti_ext[i, z, here, :], s + sti_ext[i, z + 2, here, :]),
                    (s + sti_ext[i, z + 1, down, :], s + sti_ext[i, z + 1, up, :]),
                    (s + s_minus[i], s + s_plus[i]),
                ])
            for c in range(3):
                v_mid = [ext_ref[c, i, z + WIDE, here, :] for i in range(blocks)]
                v_plus, v_minus = edges_of(v_mid)
                for i in range(blocks):
                    v = v_mid[i]
                    pairs = (
                        (ext_ref[c, i, z + WIDE - 1, here, :], ext_ref[c, i, z + WIDE + 1, here, :]),
                        (ext_ref[c, i, z + WIDE, down, :], ext_ref[c, i, z + WIDE, up, :]),
                        (v_minus[i], v_plus[i]),
                    )
                    total = None
                    for (low, high), (f_low, f_high) in zip(pairs, faces[i]):
                        part = f_low * (v - low) + f_high * (v - high)
                        total = part if total is None else total + part
                    term = (0.5 * BETA) * total
                    reg_ref[c, z, at, pl.ds(i * LANES, LANES)] = term
                    acc = acc + v * term
        return acc

    acc = lax.fori_loop(0, sections, plane, jnp.zeros((TILE, LANES), jnp.float32))
    sum_ref[...] = acc


def to_rows(scan):
    count = lax.axis_size("row")
    sections, width, rows = scan.shape
    own = rows // count
    shape = (count, sections, own, width)
    if width == LANES and rows % width == 0 and width % own == 0:
        (parts,) = call(block_kernel, [shape], [VMEM], [])(scan)
    else:
        parts = jnp.swapaxes(scan, 1, 2).reshape(sections, count, own, width).transpose(1, 0, 2, 3)
    parts = lax.all_to_all(parts, "row", split_axis=0, concat_axis=0, tiled=True)
    if width == LANES:
        return parts
    whole = parts.transpose(1, 2, 0, 3).reshape(sections, own, count * width // LANES, LANES)
    return whole.transpose(2, 0, 1, 3)


def part_shapes(shape, width):
    blocks, sections, rows, _ = shape
    return [(blocks, sections, SENT, LANES)] * 2 + [(blocks, width, rows, LANES)] * 2


def halos(low_rows, high_rows, low, high):
    width = low.shape[1]
    before, after = exchange(low_rows, high_rows, "row")
    below, above = exchange(low, high, "sec")
    corners = [
        jnp.concatenate([before[:, cut], after[:, cut]], axis=2)
        for cut in (slice(0, width), slice(before.shape[1] - width, None))
    ]
    return (below, above, before, after) + exchange(*corners, "sec")


def everywhere(part):
    for axis in ("row", "sec"):
        count, near = lax.axis_size(axis), 1
        if count & (count - 1):
            part = lax.psum(part, axis)
            continue
        while near < count:
            part = part + lax.ppermute(part, axis, [(i, i ^ near) for i in range(count)])
            near *= 2
    return part


def call(kernel, shapes, ins, scratch, flops=0, megabytes=20):
    return pl.pallas_call(
        kernel,
        out_shape=[jax.ShapeDtypeStruct(shape, jnp.float32) for shape in shapes],
        in_specs=ins,
        out_specs=[VMEM] * len(shapes),
        scratch_shapes=[pltpu.VMEM(shape, jnp.float32) for shape in scratch],
        compiler_params=pltpu.CompilerParams(vmem_limit_bytes=megabytes << 20),
        cost_estimate=pl.CostEstimate(flops=flops, bytes_accessed=4 << 20, transcendentals=0),
    )


def local(template_scan, reference_scan, velocity, stiffness):
    _, sections, rows, width = velocity.shape
    blocks = width // LANES
    tall, deep = rows + 2 * GAP, sections + 2 * WIDE
    own = (blocks, sections, rows, LANES)
    sec, row = lax.axis_index("sec"), lax.axis_index("row")
    flags = jnp.stack([
        sec > 0, sec < lax.axis_size("sec") - 1, row > 0, row < lax.axis_size("row") - 1
    ]).astype(jnp.float32)

    template = to_rows(template_scan)

    sides = [
        jnp.concatenate([velocity[:, :, cut].reshape(-1, width), stiffness[:, one]], axis=0)
        for cut, one in ((slice(0, WIDE), 0), (slice(rows - WIDE, rows), rows - 1))
    ]
    before, after = exchange(sides[0], sides[1], "row")
    planes = [
        jnp.concatenate([velocity[:, cut].reshape(-1, rows, width), stiffness[one]], axis=0)
        for cut, one in (
            (slice(0, WIDE), slice(0, 1)), (slice(sections - WIDE, sections), slice(sections - 1, sections))
        )
    ]
    below, above = exchange(planes[0], planes[1], "sec")
    corners = [
        jnp.concatenate([
            side[: 3 * sections * WIDE].reshape(3, sections, WIDE, width)[:, cut].reshape(-1, width)
            for side in (before, after)
        ], axis=0)
        for cut in (slice(0, WIDE), slice(sections - WIDE, sections))
    ]
    corners_below, corners_above = exchange(corners[0], corners[1], "sec")
    extended, reg, reg_sums = call(
        regular_kernel,
        [(3, blocks, deep, tall, LANES), velocity.shape, (TILE, LANES)],
        [VMEM] * 8,
        [(blocks, sections + 2, tall, LANES)],
        20 << 20,
    )(velocity, stiffness, below, above, before, after, corners_below, corners_above)

    parts = call(part_kernel, part_shapes(own, STEPS), [VMEM], [])(template)
    moved, *levels = call(
        forward_kernel,
        [own] + [(blocks, sections + 2 * STEPS, tall, LANES)] * STEPS,
        [SMEM] + [VMEM] * 8,
        [],
        20 << 20,
    )(flags, template, *halos(*parts), extended)

    fixed = to_rows(reference_scan)
    misfit, *parts, partial = call(
        misfit_kernel, [own] + part_shapes(own, WIDE) + [(TILE, LANES)], [VMEM] * 3, []
    )(moved, fixed, reg_sums)
    (gradient,) = call(
        adjoint_kernel,
        [velocity.shape],
        [SMEM] + [VMEM] * (9 + STEPS),
        [(blocks, deep, tall, LANES)] * STEPS,
        20 << 20,
    )(flags, misfit, *halos(*parts), extended, *levels, reg)

    voxels = sections * rows * width * lax.axis_size("sec") * lax.axis_size("row")
    objective = jnp.sum(everywhere(partial)) / voxels
    return (gradient, objective)


def solution(mesh):
    return jax.shard_map(
        local,
        mesh=mesh,
        in_specs=(
            P("sec", "row", None),
            P("sec", "row", None),
            P(None, "sec", "row", None),
            P("sec", "row", None),
        ),
        out_specs=(P(None, "sec", "row", None), P()),
        check_vma=False,
    )
```

```python
import jax
import jax.numpy as jnp
from jax import lax
from jax.experimental import pallas as pl
from jax.experimental.pallas import tpu as pltpu
from jax.sharding import PartitionSpec as P

STEPS = 4

DT = 0.25
KAPPA = 0.5
BETA = 0.5

LANES = 128
TILE = 8
GAP = 8
SENT = 4
WIDE = STEPS - 1
WEIGHT = DT * KAPPA
SELF = 1.0 - 6.0 * WEIGHT
assert WEIGHT == DT * 0.5

VMEM = pl.BlockSpec(memory_space=pltpu.VMEM)
SMEM = pl.BlockSpec(memory_space=pltpu.SMEM)
ANY = pl.BlockSpec(memory_space=pl.ANY)


def exchange(low_part, high_part, axis):
    count = lax.axis_size(axis)
    below = lax.ppermute(high_part, axis, [(i, i + 1) for i in range(count - 1)])
    above = lax.ppermute(low_part, axis, [(i + 1, i) for i in range(count - 1)])
    return below, above


def edges(tiles_up, tiles_down):
    lane = lax.broadcasted_iota(jnp.int32, tiles_up[0].shape, 1)
    zero = jnp.zeros_like(tiles_up[0])
    up = [pltpu.roll(t, LANES - 1, 1) for t in tiles_up]
    down = [pltpu.roll(t, 1, 1) for t in tiles_down]
    plus = [jnp.where(lane == LANES - 1, n, u) for u, n in zip(up, up[1:] + [zero])]
    minus = [jnp.where(lane == 0, p, d) for d, p in zip(down, [zero] + down[:-1])]
    return plus, minus


def edges_of(tiles):
    return edges(tiles, tiles)


def fill(out, own, below, above, before, after, width):
    blocks, sections, rows, _ = own.shape
    top, bottom = pl.ds(GAP - SENT, SENT), pl.ds(GAP + rows, SENT)

    def whole(z, _):
        for i in range(blocks):
            out[i, z + width, pl.ds(GAP, rows), :] = own[i, z, :, :]
            out[i, z + width, top, :] = before[i, z, :, :]
            out[i, z + width, bottom, :] = after[i, z, :, :]
        return 0

    def halo(z, _):
        for planes, at in ((below, z), (above, z + width + sections)):
            for i in range(blocks):
                out[i, at, pl.ds(GAP, rows), :] = planes[i, z, pl.ds(0, rows), :]
                out[i, at, top, :] = planes[i, z, pl.ds(rows, SENT), :]
                out[i, at, bottom, :] = planes[i, z, pl.ds(rows + SENT, SENT), :]
        return 0

    lax.fori_loop(0, sections, whole, 0)
    lax.fori_loop(0, width, halo, 0)


def block_kernel(scan, out):
    sections, width, rows = scan.shape
    own = out.shape[2]

    def section(z, _):
        for cut in range(0, rows, width):
            turned = scan[z, :, pl.ds(cut, width)].T
            for r in range(0, width, own):
                out[(cut + r) // own, z, :, :] = turned[r : r + own]
        return 0

    lax.fori_loop(0, sections, section, 0)


def end_kernel(field, gate, low_rows, high_rows):
    del gate
    blocks, sections, rows, _ = field.shape

    def section(z, _):
        for i in range(blocks):
            low_rows[i, z, :, :] = field[i, z, pl.ds(0, SENT), :]
            high_rows[i, z, :, :] = field[i, z, pl.ds(rows - SENT, SENT), :]
        return 0

    lax.fori_loop(0, sections, section, 0)


def plane_kernel(field, before, after, low, high):
    blocks, sections, rows, _ = field.shape
    width = low.shape[1]

    def plane(z, _):
        for out, at in ((low, z), (high, z + sections - width)):
            for i in range(blocks):
                out[i, z, pl.ds(0, rows), :] = field[i, at, :, :]
                out[i, z, pl.ds(rows, SENT), :] = before[i, at, :, :]
                out[i, z, pl.ds(rows + SENT, SENT), :] = after[i, at, :, :]
        return 0

    lax.fori_loop(0, width, plane, 0)


def misfit_kernel(moved, fixed, sums, misfit, low_rows, high_rows, total_ref):
    blocks, sections, rows, _ = moved.shape

    def section(z, acc):
        for i in range(blocks):
            for r in range(0, rows, TILE):
                value = moved[i, z, pl.ds(r, TILE), :] - fixed[i, z, pl.ds(r, TILE), :]
                misfit[i, z, pl.ds(r, TILE), :] = value
                acc = acc + value * value
                if r == 0:
                    low_rows[i, z, :, :] = value[:SENT]
                if r == rows - TILE:
                    high_rows[i, z, :, :] = value[TILE - SENT :]
        return acc

    zero = jnp.zeros((TILE, LANES), jnp.float32)
    total_ref[...] = 0.5 * (lax.fori_loop(0, sections, section, zero) + sums[...])


def pack_kernel(vel, sti, low_rows, high_rows, low, high):
    _, sections, rows, _ = vel.shape
    for c in range(3):
        for z in range(sections):
            at = pl.ds((c * sections + z) * WIDE, WIDE)
            low_rows[at, :] = vel[c, z, pl.ds(0, WIDE), :]
            high_rows[at, :] = vel[c, z, pl.ds(rows - WIDE, WIDE), :]
    for z in range(sections):
        at = pl.ds(3 * sections * WIDE + z, 1)
        low_rows[at, :] = sti[z, pl.ds(0, 1), :]
        high_rows[at, :] = sti[z, pl.ds(rows - 1, 1), :]

    def plane(z, _):
        for c in range(3):
            low[c * WIDE + z, :, :] = vel[c, z, :, :]
            high[c * WIDE + z, :, :] = vel[c, sections - WIDE + z, :, :]
        return 0

    lax.fori_loop(0, WIDE, plane, 0)
    low[3 * WIDE, :, :] = sti[0, :, :]
    high[3 * WIDE, :, :] = sti[sections - 1, :, :]


def corner_kernel(before, after, low, high):
    size = WIDE * WIDE
    sections = before.shape[0] // (3 * WIDE + 1)
    for c in range(3):
        for half, src in enumerate((before, after)):
            to = pl.ds((half * 3 + c) * size, size)
            low[to, :] = src[pl.ds(c * sections * WIDE, size), :]
            high[to, :] = src[pl.ds((c + 1) * sections * WIDE - size, size), :]


def groups(rows, reach):
    if reach == 0:
        return [GAP + g for g in range(0, rows, TILE)]
    return [GAP - SENT + g for g in range(0, rows + TILE, TILE)]


def masked(value, start, rows, flags):
    row = start + lax.broadcasted_iota(jnp.int32, value.shape, 0)
    if start < GAP:
        return jnp.where((row >= GAP) | (flags[2] > 0.5), value, 0.0)
    if start + TILE > GAP + rows:
        return jnp.where((row < GAP + rows) | (flags[3] > 0.5), value, 0.0)
    return value


def weights(flags, z, low, high):
    factor = jnp.where(z < low, flags[0], jnp.where(z >= high, flags[1], 1.0))
    return SELF * factor, WEIGHT * factor


def forward_kernel(flags, own, below, above, before, after, ext, moved_ref, kept, *scratch):
    levels, vel, vel_sem, kept_sem = scratch[:STEPS], scratch[STEPS], scratch[STEPS + 1], scratch[STEPS + 2]
    blocks, sections, rows, _ = own.shape

    def load(z):
        return pltpu.make_async_copy(ext.at[:, :, z], vel.at[:, :, z], vel_sem.at[z])

    for z in range(sections + 2 * WIDE):
        load(z).start()
    fill(levels[0], own, below, above, before, after, STEPS)
    copies = []
    for step in range(STEPS):
        src = levels[step]
        copies.append(
            pltpu.make_async_copy(
                src.at[:, pl.ds(STEPS - 1, sections + 2)], kept.at[step], kept_sem.at[step]
            )
        )
        copies[-1].start()
        reach = STEPS - 1 - step

        def plane(z, _, src=src, step=step, reach=reach):
            if step == 0:
                load(z - 1).wait()
            keep, weight = weights(flags, z, STEPS, STEPS + sections)
            for r in groups(rows, reach):
                here = pl.ds(r, TILE)
                mids = [src[i, z, here, :] for i in range(blocks)]
                plus, minus = edges_of(mids)
                for i in range(blocks):
                    zp, zm = src[i, z + 1, here, :], src[i, z - 1, here, :]
                    xp, xm = src[i, z, pl.ds(r + 1, TILE), :], src[i, z, pl.ds(r - 1, TILE), :]
                    yp, ym = plus[i], minus[i]
                    total = (zp + zm) - vel[0, i, z - 1, here, :] * (zp - zm)
                    total = total + ((xp + xm) - vel[1, i, z - 1, here, :] * (xp - xm))
                    total = total + ((yp + ym) - vel[2, i, z - 1, here, :] * (yp - ym))
                    value = keep * mids[i] + weight * total
                    if step == STEPS - 1:
                        moved_ref[i, z - STEPS, pl.ds(r - GAP, TILE), :] = value
                    else:
                        levels[step + 1][i, z, here, :] = masked(value, r, rows, flags)
            return 0

        lax.fori_loop(STEPS - reach, STEPS + sections + reach, plane, 0)
    for copy in copies:
        copy.wait()


def adjoint_kernel(flags, own, below, above, before, after, ext, kept_all, reg_all, grad_all, *scratch):
    levels, (vel, kept, reg, grad_ref, vel_sem, kept_sem, reg_sem, grad_sem) = scratch[:STEPS], scratch[STEPS:]
    blocks, sections, rows, _ = own.shape

    def load(z):
        return pltpu.make_async_copy(ext.at[:, :, z], vel.at[:, :, z], vel_sem.at[z])

    def save(z):
        return pltpu.make_async_copy(grad_ref.at[:, z], grad_all.at[:, z], grad_sem.at[z])

    later = [
        pltpu.make_async_copy(kept_all.at[k], kept.at[k], kept_sem.at[k]) for k in range(STEPS)
    ] + [pltpu.make_async_copy(reg_all, reg, reg_sem.at[0])]
    for z in range(sections + 2 * WIDE):
        load(z).start()
    for copy in later:
        copy.start()
    fill(levels[0], own, below, above, before, after, WIDE)
    load(0).wait()
    load(1).wait()
    for step in range(WIDE):
        src, out = levels[step], levels[step + 1]
        reach = WIDE - 1 - step

        def plane(z, _, src=src, out=out, reach=reach):
            if reach == WIDE - 1:
                load(z + 1).wait()
            keep, weight = weights(flags, z, WIDE, WIDE + sections)
            for r in groups(rows, reach):
                here, up, down = pl.ds(r, TILE), pl.ds(r + 1, TILE), pl.ds(r - 1, TILE)
                mids = [src[i, z, here, :] for i in range(blocks)]
                prods = [mids[i] * vel[2, i, z, here, :] for i in range(blocks)]
                plus, minus = edges(
                    [m + p for m, p in zip(mids, prods)], [m - p for m, p in zip(mids, prods)]
                )
                for i in range(blocks):
                    zp, zm = src[i, z + 1, here, :], src[i, z - 1, here, :]
                    xp, xm = src[i, z, up, :], src[i, z, down, :]
                    total = plus[i] + minus[i]
                    total = total + (zp + zp * vel[0, i, z + 1, here, :])
                    total = total + (zm - zm * vel[0, i, z - 1, here, :])
                    total = total + (xp + xp * vel[1, i, z, up, :])
                    total = total + (xm - xm * vel[1, i, z, down, :])
                    value = keep * mids[i] + weight * total
                    if reach > 0:
                        value = masked(value, r, rows, flags)
                    out[i, z, here, :] = value
            return 0

        lax.fori_loop(WIDE - reach, WIDE + sections + reach, plane, 0)

    for copy in later:
        copy.wait()

    def slope(z, _):
        for r in groups(rows, 0):
            here, up, down = pl.ds(r, TILE), pl.ds(r + 1, TILE), pl.ds(r - 1, TILE)
            at = pl.ds(r - GAP, TILE)
            sums = [[None] * 3 for _ in range(blocks)]
            for k in range(STEPS):
                adj = [levels[STEPS - 1 - k][i, z + WIDE, here, :] for i in range(blocks)]
                plus, minus = edges_of([kept[k, i, z + 1, here, :] for i in range(blocks)])
                for i in range(blocks):
                    parts = (
                        adj[i] * (kept[k, i, z + 2, here, :] - kept[k, i, z, here, :]),
                        adj[i] * (kept[k, i, z + 1, up, :] - kept[k, i, z + 1, down, :]),
                        adj[i] * (plus[i] - minus[i]),
                    )
                    for a in range(3):
                        sums[i][a] = parts[a] if k == 0 else sums[i][a] + parts[a]
            for i in range(blocks):
                lanes = pl.ds(i * LANES, LANES)
                for a in range(3):
                    grad_ref[a, z, at, lanes] = reg[a, z, at, lanes] - (0.5 * DT) * sums[i][a]
        save(z).start()
        return 0

    lax.fori_loop(0, sections, slope, 0)
    for z in range(sections):
        save(z).wait()


def lay(out, src, z):
    rows, width = src.shape
    for i in range(width // LANES):
        out[i, z, pl.ds(GAP, rows), :] = src[:, pl.ds(i * LANES, LANES)]


def lay_rows(out, z, row, src, at, count):
    for i in range(src.shape[1] // LANES):
        out[i, z, pl.ds(row, count), :] = src[pl.ds(at, count), pl.ds(i * LANES, LANES)]


def extend_kernel(vel, planes_below, planes_above, before, after, corners_below, corners_above, ext_ref):
    _, sections, rows, _ = vel.shape

    def mid(z, _):
        for c in range(3):
            lay(ext_ref.at[c], vel.at[c, z], z + WIDE)
        return 0

    def far(z, _):
        for c in range(3):
            lay(ext_ref.at[c], planes_below.at[c * WIDE + z], z)
            lay(ext_ref.at[c], planes_above.at[c * WIDE + z], z + WIDE + sections)
        return 0

    lax.fori_loop(0, sections, mid, 0)
    lax.fori_loop(0, WIDE, far, 0)
    low, high = GAP - WIDE, GAP + rows
    for c in range(3):
        for z in range(sections):
            at = (c * sections + z) * WIDE
            lay_rows(ext_ref.at[c], z + WIDE, low, before, at, WIDE)
            lay_rows(ext_ref.at[c], z + WIDE, high, after, at, WIDE)
        for z in range(WIDE):
            at, half = (c * WIDE + z) * WIDE, 3 * WIDE * WIDE
            for src, z_out in ((corners_below, z), (corners_above, z + WIDE + sections)):
                lay_rows(ext_ref.at[c], z_out, low, src, at, WIDE)
                lay_rows(ext_ref.at[c], z_out, high, src, at + half, WIDE)


def regular_kernel(gate, ext_ref, sti, planes_below, planes_above, before, after, reg_ref, sum_ref, sti_ext):
    del gate
    sections, rows, width = sti.shape
    blocks = width // LANES

    def mid(z, _):
        lay(sti_ext, sti.at[z], z + 1)
        return 0

    lax.fori_loop(0, sections, mid, 0)
    lay(sti_ext, planes_below.at[3 * WIDE], 0)
    lay(sti_ext, planes_above.at[3 * WIDE], sections + 1)
    for z in range(sections):
        at = 3 * sections * WIDE + z
        lay_rows(sti_ext, z + 1, GAP - 1, before, at, 1)
        lay_rows(sti_ext, z + 1, GAP + rows, after, at, 1)

    def plane(z, acc):
        for r in groups(rows, 0):
            here, up, down = pl.ds(r, TILE), pl.ds(r + 1, TILE), pl.ds(r - 1, TILE)
            at = pl.ds(r - GAP, TILE)
            s_mid = [sti_ext[i, z + 1, here, :] for i in range(blocks)]
            s_plus, s_minus = edges_of(s_mid)
            faces = []
            for i in range(blocks):
                s = s_mid[i]
                faces.append([
                    (s + sti_ext[i, z, here, :], s + sti_ext[i, z + 2, here, :]),
                    (s + sti_ext[i, z + 1, down, :], s + sti_ext[i, z + 1, up, :]),
                    (s + s_minus[i], s + s_plus[i]),
                ])
            for c in range(3):
                v_mid = [ext_ref[c, i, z + WIDE, here, :] for i in range(blocks)]
                v_plus, v_minus = edges_of(v_mid)
                for i in range(blocks):
                    v = v_mid[i]
                    pairs = (
                        (ext_ref[c, i, z + WIDE - 1, here, :], ext_ref[c, i, z + WIDE + 1, here, :]),
                        (ext_ref[c, i, z + WIDE, down, :], ext_ref[c, i, z + WIDE, up, :]),
                        (v_minus[i], v_plus[i]),
                    )
                    total = None
                    for (low, high), (f_low, f_high) in zip(pairs, faces[i]):
                        part = f_low * (v - low) + f_high * (v - high)
                        total = part if total is None else total + part
                    term = (0.5 * BETA) * total
                    reg_ref[c, z, at, pl.ds(i * LANES, LANES)] = term
                    acc = acc + v * term
        return acc

    acc = lax.fori_loop(0, sections, plane, jnp.zeros((TILE, LANES), jnp.float32))
    sum_ref[...] = acc


def after(value, *gates):
    def kernel(*refs):
        del refs

    return pl.pallas_call(
        kernel,
        out_shape=jax.ShapeDtypeStruct(value.shape, value.dtype),
        in_specs=[ANY] * (1 + len(gates)),
        out_specs=ANY,
        input_output_aliases={0: 0},
    )(value, *gates)


def to_blocks(scan):
    count = lax.axis_size("row")
    sections, width, rows = scan.shape
    own = rows // count
    if width == LANES and rows % width == 0 and width % own == 0:
        return call(block_kernel, [(count, sections, own, width)], [VMEM])(scan)[0]
    return jnp.swapaxes(scan, 1, 2).reshape(sections, count, own, width).transpose(1, 0, 2, 3)


def to_rows(parts):
    parts = lax.all_to_all(parts, "row", split_axis=0, concat_axis=0, tiled=True)
    count, sections, own, width = parts.shape
    if width == LANES:
        return parts
    whole = parts.transpose(1, 2, 0, 3).reshape(sections, own, count * width // LANES, LANES)
    return whole.transpose(2, 0, 1, 3)


def halos(field, width, low_rows, high_rows):
    blocks, _, rows, _ = field.shape
    before, after_ = exchange(low_rows, high_rows, "row")
    low, high = call(plane_kernel, [(blocks, width, rows + 2 * SENT, LANES)] * 2, [VMEM] * 3)(
        field, before, after_
    )
    return exchange(low, high, "sec") + (before, after_)


def everywhere(part):
    for axis in ("row", "sec"):
        count, near = lax.axis_size(axis), 1
        if count & (count - 1):
            part = lax.psum(part, axis)
            continue
        while near < count:
            part = part + lax.ppermute(part, axis, [(i, i ^ near) for i in range(count)])
            near *= 2
    return part


def call(kernel, shapes, ins, scratch=(), outs=None, flops=0):
    return pl.pallas_call(
        kernel,
        out_shape=[jax.ShapeDtypeStruct(shape, jnp.float32) for shape in shapes],
        in_specs=ins,
        out_specs=outs or [VMEM] * len(shapes),
        scratch_shapes=[
            pltpu.VMEM(shape, jnp.float32) if isinstance(shape, tuple) else pltpu.SemaphoreType.DMA((shape,))
            for shape in scratch
        ],
        compiler_params=pltpu.CompilerParams(vmem_limit_bytes=63 << 20),
        cost_estimate=pl.CostEstimate(flops=flops, bytes_accessed=4 << 20, transcendentals=0),
    )


def local(template_scan, reference_scan, velocity, stiffness):
    _, sections, rows, width = velocity.shape
    blocks = width // LANES
    tall, deep = rows + 2 * GAP, sections + 2 * WIDE
    own = (blocks, sections, rows, LANES)
    ends = (blocks, sections, SENT, LANES)
    sec, row = lax.axis_index("sec"), lax.axis_index("row")
    flags = jnp.stack([
        sec > 0, sec < lax.axis_size("sec") - 1, row > 0, row < lax.axis_size("row") - 1
    ]).astype(jnp.float32)

    template = to_rows(to_blocks(template_scan))

    lines = (3 * WIDE + 1) * sections
    low_rows, high_rows, low, high = call(
        pack_kernel, [(lines, width)] * 2 + [(3 * WIDE + 1, rows, width)] * 2, [VMEM] * 2
    )(velocity, stiffness)
    before, after_ = exchange(low_rows, high_rows, "row")
    below, above = exchange(low, high, "sec")
    corners = call(corner_kernel, [(6 * WIDE * WIDE, width)] * 2, [VMEM] * 2)(before, after_)
    (extended,) = call(extend_kernel, [(3, blocks, deep, tall, LANES)], [VMEM] * 7)(
        velocity, below, above, before, after_, *exchange(*corners, "sec")
    )

    parts = call(end_kernel, [ends] * 2, [VMEM, ANY])(template, extended)
    fixed = to_rows(after(to_blocks(reference_scan), parts[0]))
    level = (blocks, sections + 2 * STEPS, tall, LANES)
    moved, kept = call(
        forward_kernel,
        [own, (STEPS, blocks, sections + 2, tall, LANES)],
        [SMEM] + [VMEM] * 5 + [ANY],
        [level] * STEPS + [(3, blocks, deep, tall, LANES), deep, STEPS],
        [VMEM, ANY],
        20 << 20,
    )(flags, template, *halos(template, STEPS, *parts), extended)

    reg, reg_sums = call(
        regular_kernel,
        [velocity.shape, (TILE, LANES)],
        [ANY] + [VMEM] * 6,
        [(blocks, sections + 2, tall, LANES)],
        flops=20 << 20,
    )(moved, extended, stiffness, below, above, before, after_)

    misfit, *parts, partial = call(misfit_kernel, [own, ends, ends, (TILE, LANES)], [VMEM] * 3)(
        moved, fixed, reg_sums
    )
    around = halos(misfit, WIDE, *parts)
    (gradient,) = call(
        adjoint_kernel,
        [velocity.shape],
        [SMEM] + [VMEM] * 5 + [ANY] * 3,
        [(blocks, deep, tall, LANES)] * STEPS
        + [(3, blocks, deep, tall, LANES), (STEPS, blocks, sections + 2, tall, LANES)]
        + [velocity.shape] * 2 + [deep, STEPS, 1, sections],
        [ANY],
        20 << 20,
    )(flags, misfit, *around, extended, kept, reg)

    voxels = sections * rows * width * lax.axis_size("sec") * lax.axis_size("row")
    objective = jnp.sum(everywhere(after(partial, around[2], around[3]))) / voxels
    return (gradient, objective)


def solution(mesh):
    return jax.shard_map(
        local,
        mesh=mesh,
        in_specs=(
            P("sec", "row", None),
            P("sec", "row", None),
            P(None, "sec", "row", None),
            P("sec", "row", None),
        ),
        out_specs=(P(None, "sec", "row", None), P()),
        check_vma=False,
    )
```

```python
import jax
import jax.numpy as jnp
from jax import lax
from jax.experimental import pallas as pl
from jax.experimental.pallas import tpu as pltpu
from jax.sharding import PartitionSpec as P

STEPS = 4

DT = 0.25
KAPPA = 0.5
BETA = 0.5

LANES = 128
TILE = 8
GAP = 4
SENT = 4
WIDE = STEPS - 1
WEIGHT = DT * KAPPA
SELF = 1.0 - 6.0 * WEIGHT
assert WEIGHT == DT * 0.5

VMEM = pl.BlockSpec(memory_space=pltpu.VMEM)
SMEM = pl.BlockSpec(memory_space=pltpu.SMEM)
ANY = pl.BlockSpec(memory_space=pl.ANY)


def exchange(low_part, high_part, axis):
    count = lax.axis_size(axis)
    below = lax.ppermute(high_part, axis, [(i, i + 1) for i in range(count - 1)])
    above = lax.ppermute(low_part, axis, [(i + 1, i) for i in range(count - 1)])
    return below, above


def edges(tiles_up, tiles_down):
    lane = lax.broadcasted_iota(jnp.int32, tiles_up[0].shape, 1)
    zero = jnp.zeros_like(tiles_up[0])
    up = [pltpu.roll(t, LANES - 1, 1) for t in tiles_up]
    down = [pltpu.roll(t, 1, 1) for t in tiles_down]
    plus = [jnp.where(lane == LANES - 1, n, u) for u, n in zip(up, up[1:] + [zero])]
    minus = [jnp.where(lane == 0, p, d) for d, p in zip(down, [zero] + down[:-1])]
    return plus, minus


def edges_of(tiles):
    return edges(tiles, tiles)


def fill(out, own, below, above, before, after, width):
    blocks, sections, rows, _ = own.shape

    def whole(z, _):
        for i in range(blocks):
            out[i, z + width, pl.ds(GAP, rows), :] = own[i, z, :, :]
            out[i, z + width, pl.ds(0, SENT), :] = before[i, z, :, :]
            out[i, z + width, pl.ds(GAP + rows, SENT), :] = after[i, z, :, :]
        return 0

    def halo(z, _):
        for planes, at in ((below, z), (above, z + width + sections)):
            for i in range(blocks):
                out[i, at, :, :] = planes[i, z, :, :]
        return 0

    lax.fori_loop(0, sections, whole, 0)
    lax.fori_loop(0, width, halo, 0)


def block_kernel(scan, gate, out, turned):
    del gate
    sections, width, rows = scan.shape
    count, _, tall, _ = out.shape
    own = rows // count
    first = TILE - (tall - own) // 2
    zero = jnp.zeros((TILE, width), jnp.float32)
    turned[pl.ds(0, TILE), :] = zero
    turned[pl.ds(TILE + rows, TILE), :] = zero

    def section(z, _):
        for cut in range(0, rows, width):
            turned[pl.ds(TILE + cut, width), :] = scan[z, :, pl.ds(cut, width)].T
        for j in range(count):
            out[j, z, :, :] = turned[pl.ds(first + j * own, tall), :]
        return 0

    lax.fori_loop(0, sections, section, 0)


def slice_kernel(field, low, high, sem):
    sections, width = field.shape[1], low.shape[1]
    copies = [
        pltpu.make_async_copy(field.at[:, pl.ds(0, width)], low, sem.at[0]),
        pltpu.make_async_copy(field.at[:, pl.ds(sections - width, width)], high, sem.at[1]),
    ]
    for copy in copies:
        copy.start()
    for copy in copies:
        copy.wait()


def plane_kernel(field, before, after, low, high):
    blocks, sections, rows, _ = field.shape
    width = low.shape[1]

    def plane(z, _):
        for out, at in ((low, z), (high, z + sections - width)):
            for i in range(blocks):
                out[i, z, pl.ds(0, SENT), :] = before[i, at, :, :]
                out[i, z, pl.ds(GAP, rows), :] = field[i, at, :, :]
                out[i, z, pl.ds(GAP + rows, SENT), :] = after[i, at, :, :]
        return 0

    lax.fori_loop(0, width, plane, 0)


def misfit_kernel(moved, fixed, sums, misfit, low_rows, high_rows, total_ref):
    blocks, sections, rows, _ = moved.shape

    def section(z, acc):
        for i in range(blocks):
            for r in range(0, rows, TILE):
                value = moved[i, z, pl.ds(r, TILE), :] - fixed[i, z, pl.ds(r, TILE), :]
                misfit[i, z, pl.ds(r, TILE), :] = value
                acc = acc + value * value
                if r == 0:
                    low_rows[i, z, :, :] = value[:SENT]
                if r == rows - TILE:
                    high_rows[i, z, :, :] = value[TILE - SENT :]
        return acc

    zero = jnp.zeros((TILE, LANES), jnp.float32)
    total_ref[...] = 0.5 * (lax.fori_loop(0, sections, section, zero) + sums[...])


def pack_kernel(vel, sti, low_rows, high_rows, low, high, sem):
    _, sections, rows, _ = vel.shape
    copies = []
    for half, (out, at, one) in enumerate(((low, 0, 0), (high, sections - WIDE, sections - 1))):
        for c in range(3):
            copies.append(pltpu.make_async_copy(
                vel.at[c, pl.ds(at, WIDE)], out.at[pl.ds(c * WIDE, WIDE)], sem.at[4 * half + c]
            ))
        copies.append(pltpu.make_async_copy(
            sti.at[pl.ds(one, 1)], out.at[pl.ds(3 * WIDE, 1)], sem.at[4 * half + 3]
        ))
    for copy in copies:
        copy.start()
    for c in range(3):
        for z in range(sections):
            at = pl.ds((c * sections + z) * WIDE, WIDE)
            low_rows[at, :] = vel[c, z, pl.ds(0, WIDE), :]
            high_rows[at, :] = vel[c, z, pl.ds(rows - WIDE, WIDE), :]
    for z in range(sections):
        at = pl.ds(3 * sections * WIDE + z, 1)
        low_rows[at, :] = sti[z, pl.ds(0, 1), :]
        high_rows[at, :] = sti[z, pl.ds(rows - 1, 1), :]
    for copy in copies:
        copy.wait()


def corner_kernel(before, after, low, high):
    size = WIDE * WIDE
    sections = before.shape[0] // (3 * WIDE + 1)
    for c in range(3):
        for half, src in enumerate((before, after)):
            to = pl.ds((half * 3 + c) * size, size)
            low[to, :] = src[pl.ds(c * sections * WIDE, size), :]
            high[to, :] = src[pl.ds((c + 1) * sections * WIDE - size, size), :]


def groups(rows, reach):
    if reach == 0:
        return [GAP + g for g in range(0, rows, TILE)]
    return [1 + g for g in range(0, rows, TILE)] + [rows + 2 * GAP - 1 - TILE]


def masked(value, start, rows, flags):
    row = start + lax.broadcasted_iota(jnp.int32, value.shape, 0)
    if start < GAP:
        return jnp.where((row >= GAP) | (flags[2] > 0.5), value, 0.0)
    if start + TILE > GAP + rows:
        return jnp.where((row < GAP + rows) | (flags[3] > 0.5), value, 0.0)
    return value


def weights(flags, z, low, high):
    factor = jnp.where(z < low, flags[0], jnp.where(z >= high, flags[1], 1.0))
    return SELF * factor, WEIGHT * factor


def forward_kernel(flags, own, below, above, ext, moved_ref, kept, *scratch):
    levels, (vel, own_sem, vel_sem, kept_sem) = scratch[:STEPS], scratch[STEPS:]
    blocks, sections, rows, _ = moved_ref.shape
    first = [
        pltpu.make_async_copy(src, levels[0].at[:, pl.ds(at, src.shape[1])], own_sem.at[n])
        for n, (src, at) in enumerate(((below, 0), (own, STEPS), (above, STEPS + sections)))
    ]

    def load(z):
        return pltpu.make_async_copy(ext.at[:, :, z], vel.at[:, :, z], vel_sem.at[z])

    for copy in first:
        copy.start()
    for z in range(sections + 2 * WIDE):
        load(z).start()
    for copy in first:
        copy.wait()
    copies = []
    for step in range(STEPS):
        src = levels[step]
        if step > 0:
            copies.append(
                pltpu.make_async_copy(
                    src.at[:, pl.ds(STEPS - 1, sections + 2)], kept.at[step - 1], kept_sem.at[step - 1]
                )
            )
            copies[-1].start()
        reach = STEPS - 1 - step

        def plane(z, _, src=src, step=step, reach=reach):
            if step == 0:
                load(z - 1).wait()
            keep, weight = weights(flags, z, STEPS, STEPS + sections)
            for r in groups(rows, reach):
                here = pl.ds(r, TILE)
                mids = [src[i, z, here, :] for i in range(blocks)]
                plus, minus = edges_of(mids)
                for i in range(blocks):
                    zp, zm = src[i, z + 1, here, :], src[i, z - 1, here, :]
                    xp, xm = src[i, z, pl.ds(r + 1, TILE), :], src[i, z, pl.ds(r - 1, TILE), :]
                    yp, ym = plus[i], minus[i]
                    total = (zp + zm) - vel[0, i, z - 1, here, :] * (zp - zm)
                    total = total + ((xp + xm) - vel[1, i, z - 1, here, :] * (xp - xm))
                    total = total + ((yp + ym) - vel[2, i, z - 1, here, :] * (yp - ym))
                    value = keep * mids[i] + weight * total
                    if step == STEPS - 1:
                        moved_ref[i, z - STEPS, pl.ds(r - GAP, TILE), :] = value
                    else:
                        levels[step + 1][i, z, here, :] = masked(value, r, rows, flags)
            return 0

        lax.fori_loop(STEPS - reach, STEPS + sections + reach, plane, 0)
    for copy in copies:
        copy.wait()


def adjoint_kernel(flags, own, below, above, before, after, ext, start, start_below, start_above,
                   kept_all, reg_all, gate, grad_all, *scratch):
    del gate
    levels, (vel, kept, reg, grad_ref, vel_sem, kept_sem, reg_sem, grad_sem) = scratch[:STEPS], scratch[STEPS:]
    blocks, sections, rows, _ = own.shape

    def load(z):
        return pltpu.make_async_copy(ext.at[:, :, z], vel.at[:, :, z], vel_sem.at[z])

    def save(z):
        return pltpu.make_async_copy(grad_ref.at[:, z], grad_all.at[:, z], grad_sem.at[z])

    later = [
        pltpu.make_async_copy(src, kept.at[0, :, pl.ds(at, src.shape[1])], kept_sem.at[STEPS - 1 + n])
        for n, (src, at) in enumerate((
            (start_below.at[:, pl.ds(STEPS - 1, 1)], 0),
            (start, 1),
            (start_above.at[:, pl.ds(0, 1)], sections + 1),
        ))
    ] + [
        pltpu.make_async_copy(kept_all.at[k], kept.at[k + 1], kept_sem.at[k]) for k in range(STEPS - 1)
    ] + [pltpu.make_async_copy(reg_all, reg, reg_sem.at[0])]
    for z in range(sections + 2 * WIDE):
        load(z).start()
    for copy in later:
        copy.start()
    fill(levels[0], own, below, above, before, after, WIDE)
    load(0).wait()
    load(1).wait()
    for step in range(WIDE):
        src, out = levels[step], levels[step + 1]
        reach = WIDE - 1 - step

        def plane(z, _, src=src, out=out, reach=reach):
            if reach == WIDE - 1:
                load(z + 1).wait()
            keep, weight = weights(flags, z, WIDE, WIDE + sections)
            for r in groups(rows, reach):
                here, up, down = pl.ds(r, TILE), pl.ds(r + 1, TILE), pl.ds(r - 1, TILE)
                mids = [src[i, z, here, :] for i in range(blocks)]
                prods = [mids[i] * vel[2, i, z, here, :] for i in range(blocks)]
                plus, minus = edges(
                    [m + p for m, p in zip(mids, prods)], [m - p for m, p in zip(mids, prods)]
                )
                for i in range(blocks):
                    zp, zm = src[i, z + 1, here, :], src[i, z - 1, here, :]
                    xp, xm = src[i, z, up, :], src[i, z, down, :]
                    total = plus[i] + minus[i]
                    total = total + (zp + zp * vel[0, i, z + 1, here, :])
                    total = total + (zm - zm * vel[0, i, z - 1, here, :])
                    total = total + (xp + xp * vel[1, i, z, up, :])
                    total = total + (xm - xm * vel[1, i, z, down, :])
                    value = keep * mids[i] + weight * total
                    if reach > 0:
                        value = masked(value, r, rows, flags)
                    out[i, z, here, :] = value
            return 0

        lax.fori_loop(WIDE - reach, WIDE + sections + reach, plane, 0)

    for copy in later:
        copy.wait()

    def slope(z, _):
        for r in groups(rows, 0):
            here, up, down = pl.ds(r, TILE), pl.ds(r + 1, TILE), pl.ds(r - 1, TILE)
            at = pl.ds(r - GAP, TILE)
            sums = [[None] * 3 for _ in range(blocks)]
            for k in range(STEPS):
                adj = [levels[STEPS - 1 - k][i, z + WIDE, here, :] for i in range(blocks)]
                plus, minus = edges_of([kept[k, i, z + 1, here, :] for i in range(blocks)])
                for i in range(blocks):
                    parts = (
                        adj[i] * (kept[k, i, z + 2, here, :] - kept[k, i, z, here, :]),
                        adj[i] * (kept[k, i, z + 1, up, :] - kept[k, i, z + 1, down, :]),
                        adj[i] * (plus[i] - minus[i]),
                    )
                    for a in range(3):
                        sums[i][a] = parts[a] if k == 0 else sums[i][a] + parts[a]
            for i in range(blocks):
                lanes = pl.ds(i * LANES, LANES)
                for a in range(3):
                    grad_ref[a, z, at, lanes] = reg[a, z, at, lanes] - (0.5 * DT) * sums[i][a]
        save(z).start()
        return 0

    lax.fori_loop(0, sections, slope, 0)
    for z in range(sections):
        save(z).wait()


def lay(out, src, z):
    rows, width = src.shape
    for i in range(width // LANES):
        out[i, z, pl.ds(GAP, rows), :] = src[:, pl.ds(i * LANES, LANES)]


def lay_rows(out, z, row, src, at, count):
    for i in range(src.shape[1] // LANES):
        out[i, z, pl.ds(row, count), :] = src[pl.ds(at, count), pl.ds(i * LANES, LANES)]


def extend_kernel(vel, planes_below, planes_above, before, after, corners_below, corners_above, ext_ref):
    _, sections, rows, _ = vel.shape

    def mid(z, _):
        for c in range(3):
            lay(ext_ref.at[c], vel.at[c, z], z + WIDE)
        return 0

    def far(z, _):
        for c in range(3):
            lay(ext_ref.at[c], planes_below.at[c * WIDE + z], z)
            lay(ext_ref.at[c], planes_above.at[c * WIDE + z], z + WIDE + sections)
        return 0

    lax.fori_loop(0, sections, mid, 0)
    lax.fori_loop(0, WIDE, far, 0)
    low, high = GAP - WIDE, GAP + rows
    for c in range(3):
        for z in range(sections):
            at = (c * sections + z) * WIDE
            lay_rows(ext_ref.at[c], z + WIDE, low, before, at, WIDE)
            lay_rows(ext_ref.at[c], z + WIDE, high, after, at, WIDE)
        for z in range(WIDE):
            at, half = (c * WIDE + z) * WIDE, 3 * WIDE * WIDE
            for src, z_out in ((corners_below, z), (corners_above, z + WIDE + sections)):
                lay_rows(ext_ref.at[c], z_out, low, src, at, WIDE)
                lay_rows(ext_ref.at[c], z_out, high, src, at + half, WIDE)


def regular_kernel(gate, ext_ref, sti, planes_below, planes_above, before, after, reg_ref, sum_ref, sti_ext):
    del gate
    sections, rows, width = sti.shape
    blocks = width // LANES

    def mid(z, _):
        lay(sti_ext, sti.at[z], z + 1)
        return 0

    lax.fori_loop(0, sections, mid, 0)
    lay(sti_ext, planes_below.at[3 * WIDE], 0)
    lay(sti_ext, planes_above.at[3 * WIDE], sections + 1)
    for z in range(sections):
        at = 3 * sections * WIDE + z
        lay_rows(sti_ext, z + 1, GAP - 1, before, at, 1)
        lay_rows(sti_ext, z + 1, GAP + rows, after, at, 1)

    def plane(z, acc):
        for r in groups(rows, 0):
            here, up, down = pl.ds(r, TILE), pl.ds(r + 1, TILE), pl.ds(r - 1, TILE)
            at = pl.ds(r - GAP, TILE)
            s_mid = [sti_ext[i, z + 1, here, :] for i in range(blocks)]
            s_plus, s_minus = edges_of(s_mid)
            faces = []
            for i in range(blocks):
                s = s_mid[i]
                faces.append([
                    (s + sti_ext[i, z, here, :], s + sti_ext[i, z + 2, here, :]),
                    (s + sti_ext[i, z + 1, down, :], s + sti_ext[i, z + 1, up, :]),
                    (s + s_minus[i], s + s_plus[i]),
                ])
            for c in range(3):
                v_mid = [ext_ref[c, i, z + WIDE, here, :] for i in range(blocks)]
                v_plus, v_minus = edges_of(v_mid)
                for i in range(blocks):
                    v = v_mid[i]
                    pairs = (
                        (ext_ref[c, i, z + WIDE - 1, here, :], ext_ref[c, i, z + WIDE + 1, here, :]),
                        (ext_ref[c, i, z + WIDE, down, :], ext_ref[c, i, z + WIDE, up, :]),
                        (v_minus[i], v_plus[i]),
                    )
                    total = None
                    for (low, high), (f_low, f_high) in zip(pairs, faces[i]):
                        part = f_low * (v - low) + f_high * (v - high)
                        total = part if total is None else total + part
                    term = (0.5 * BETA) * total
                    reg_ref[c, z, at, pl.ds(i * LANES, LANES)] = term
                    acc = acc + v * term
        return acc

    acc = lax.fori_loop(0, sections, plane, jnp.zeros((TILE, LANES), jnp.float32))
    sum_ref[...] = acc


def after(value, *gates):
    def kernel(*refs):
        del refs

    return pl.pallas_call(
        kernel,
        out_shape=jax.ShapeDtypeStruct(value.shape, value.dtype),
        in_specs=[ANY] * (1 + len(gates)),
        out_specs=ANY,
        input_output_aliases={0: 0},
    )(value, *gates)


def to_blocks(scan, extra, gate):
    count = lax.axis_size("row")
    sections, width, rows = scan.shape
    own = rows // count
    tall = own + 2 * extra
    if width == LANES and rows % width == 0:
        return call(
            block_kernel, [(count, sections, tall, width)], [VMEM, ANY], [(rows + 2 * TILE, width)]
        )(scan, gate)[0]
    turned = jnp.pad(jnp.swapaxes(scan, 1, 2), ((0, 0), (extra, extra), (0, 0)))
    return jnp.stack([turned[:, j * own : j * own + tall] for j in range(count)])


def to_rows(parts):
    parts = lax.all_to_all(parts, "row", split_axis=0, concat_axis=0, tiled=True)
    count, sections, own, width = parts.shape
    if width == LANES:
        return parts
    whole = parts.transpose(1, 2, 0, 3).reshape(sections, own, count * width // LANES, LANES)
    return whole.transpose(2, 0, 1, 3)


def summed(part, axis, lows):
    count = lax.axis_size(axis)
    got = [lax.ppermute(part, axis, [(i, i ^ low) for i in range(count)]) for low in lows]
    if len(got) == 3:
        place = lax.axis_index(axis) // lows[0] % 4
        pairs = (part + got[0], got[1] + got[2])
        return jnp.where(place < 2, pairs[0], pairs[1]) + jnp.where(place < 2, pairs[1], pairs[0])
    return part + got[0]


def stages(axis):
    count, near, found = lax.axis_size(axis), 1, []
    while near < count:
        if count % (4 * near) == 0:
            found.append((axis, (near, 2 * near, 3 * near)))
            near *= 4
        else:
            found.append((axis, (near,)))
            near *= 2
    return found


def call(kernel, shapes, ins, scratch=(), outs=None, flops=0):
    return pl.pallas_call(
        kernel,
        out_shape=[jax.ShapeDtypeStruct(shape, jnp.float32) for shape in shapes],
        in_specs=ins,
        out_specs=outs or [VMEM] * len(shapes),
        scratch_shapes=[
            pltpu.VMEM(shape, jnp.float32) if isinstance(shape, tuple) else pltpu.SemaphoreType.DMA((shape,))
            for shape in scratch
        ],
        compiler_params=pltpu.CompilerParams(vmem_limit_bytes=63 << 20),
        cost_estimate=pl.CostEstimate(flops=flops, bytes_accessed=4 << 20, transcendentals=0),
    )


def local(template_scan, reference_scan, velocity, stiffness):
    _, sections, rows, width = velocity.shape
    blocks = width // LANES
    tall, deep = rows + 2 * GAP, sections + 2 * WIDE
    own = (blocks, sections, rows, LANES)
    ends = (blocks, sections, SENT, LANES)
    sec, row = lax.axis_index("sec"), lax.axis_index("row")
    flags = jnp.stack([
        sec > 0, sec < lax.axis_size("sec") - 1, row > 0, row < lax.axis_size("row") - 1
    ]).astype(jnp.float32)

    lines = (3 * WIDE + 1) * sections
    low_rows, high_rows, low, high = call(
        pack_kernel,
        [(lines, width)] * 2 + [(3 * WIDE + 1, rows, width)] * 2,
        [VMEM] * 2,
        [8],
        [VMEM] * 2 + [ANY] * 2,
    )(velocity, stiffness)
    before, after_ = exchange(low_rows, high_rows, "row")
    template = to_rows(to_blocks(template_scan, SENT, low_rows))
    below, above = exchange(low, high, "sec")
    corners = call(corner_kernel, [(6 * WIDE * WIDE, width)] * 2, [VMEM] * 2)(before, after_)
    (extended,) = call(extend_kernel, [(3, blocks, deep, tall, LANES)], [VMEM] * 7)(
        velocity, below, above, before, after_, *exchange(*corners, "sec")
    )

    fixed_blocks = to_blocks(reference_scan, 0, corners[0])
    low, high = call(slice_kernel, [(blocks, STEPS, tall, LANES)] * 2, [ANY], [2], [ANY] * 2)(template)
    start = (template,) + exchange(low, high, "sec")
    fixed = to_rows(after(fixed_blocks, low))
    level = (blocks, sections + 2 * STEPS, tall, LANES)
    moved, kept = call(
        forward_kernel,
        [own, (STEPS - 1, blocks, sections + 2, tall, LANES)],
        [SMEM] + [ANY] * 4,
        [level] * STEPS + [(3, blocks, deep, tall, LANES), 3, deep, STEPS - 1],
        [VMEM, ANY],
        20 << 20,
    )(flags, *start, extended)

    reg, reg_sums = call(
        regular_kernel,
        [velocity.shape, (TILE, LANES)],
        [ANY] + [VMEM] * 6,
        [(blocks, sections + 2, tall, LANES)],
        flops=20 << 20,
    )(moved, extended, stiffness, below, above, before, after_)

    misfit, low_rows, high_rows, partial = call(misfit_kernel, [own, ends, ends, (TILE, LANES)], [VMEM] * 3)(
        moved, fixed, reg_sums
    )
    before, after_ = exchange(low_rows, high_rows, "row")
    low, high = call(plane_kernel, [(blocks, WIDE, tall, LANES)] * 2, [VMEM] * 3)(misfit, before, after_)
    below, above = exchange(low, high, "sec")
    partial = after(partial, low)
    for stage in stages("row"):
        partial = summed(partial, *stage)
    partial = after(partial, below, above)
    (gradient,) = call(
        adjoint_kernel,
        [velocity.shape],
        [SMEM] + [VMEM] * 5 + [ANY] * 7,
        [(blocks, deep, tall, LANES)] * STEPS
        + [(3, blocks, deep, tall, LANES), (STEPS, blocks, sections + 2, tall, LANES)]
        + [velocity.shape] * 2 + [deep, STEPS + 2, 1, sections],
        [ANY],
        20 << 20,
    )(flags, misfit, below, above, before, after_, extended, *start, kept, reg, partial)
    for stage in stages("sec"):
        partial = summed(partial, *stage)

    voxels = sections * rows * width * lax.axis_size("sec") * lax.axis_size("row")
    objective = jnp.sum(partial) / voxels
    return (gradient, objective)


def solution(mesh):
    return jax.shard_map(
        local,
        mesh=mesh,
        in_specs=(
            P("sec", "row", None),
            P("sec", "row", None),
            P(None, "sec", "row", None),
            P("sec", "row", None),
        ),
        out_specs=(P(None, "sec", "row", None), P()),
        check_vma=False,
    )
```

```python
import jax
import jax.numpy as jnp
from jax import lax
from jax.experimental import pallas as pl
from jax.experimental.pallas import tpu as pltpu
from jax.sharding import PartitionSpec as P

STEPS = 4

DT = 0.25
KAPPA = 0.5
BETA = 0.5

LANES = 128
TILE = 8
GAP = 4
SENT = 4
WIDE = STEPS - 1
WEIGHT = DT * KAPPA
SELF = 1.0 - 6.0 * WEIGHT
assert WEIGHT == DT * 0.5

VMEM = pl.BlockSpec(memory_space=pltpu.VMEM)
SMEM = pl.BlockSpec(memory_space=pltpu.SMEM)
ANY = pl.BlockSpec(memory_space=pl.ANY)


def exchange(low_part, high_part, axis):
    count = lax.axis_size(axis)
    below = lax.ppermute(high_part, axis, [(i, i + 1) for i in range(count - 1)])
    above = lax.ppermute(low_part, axis, [(i + 1, i) for i in range(count - 1)])
    return below, above


def edges(tiles_up, tiles_down):
    lane = lax.broadcasted_iota(jnp.int32, tiles_up[0].shape, 1)
    zero = jnp.zeros_like(tiles_up[0])
    up = [pltpu.roll(t, LANES - 1, 1) for t in tiles_up]
    down = [pltpu.roll(t, 1, 1) for t in tiles_down]
    plus = [jnp.where(lane == LANES - 1, n, u) for u, n in zip(up, up[1:] + [zero])]
    minus = [jnp.where(lane == 0, p, d) for d, p in zip(down, [zero] + down[:-1])]
    return plus, minus


def edges_of(tiles):
    return edges(tiles, tiles)


def fill(out, own, below, above, before, after, width):
    blocks, sections, rows, _ = own.shape

    def whole(z, _):
        for i in range(blocks):
            out[i, z + width, pl.ds(GAP, rows), :] = own[i, z, :, :]
            out[i, z + width, pl.ds(0, SENT), :] = before[i, z, :, :]
            out[i, z + width, pl.ds(GAP + rows, SENT), :] = after[i, z, :, :]
        return 0

    def halo(z, _):
        for planes, at in ((below, z), (above, z + width + sections)):
            for i in range(blocks):
                out[i, at, :, :] = planes[i, z, :, :]
        return 0

    lax.fori_loop(0, sections, whole, 0)
    lax.fori_loop(0, width, halo, 0)


def block_kernel(scan, gate, out, turned):
    del gate
    sections, width, rows = scan.shape
    count, _, tall, _ = out.shape
    own = rows // count
    first = TILE - (tall - own) // 2
    zero = jnp.zeros((TILE, width), jnp.float32)
    turned[pl.ds(0, TILE), :] = zero
    turned[pl.ds(TILE + rows, TILE), :] = zero

    def section(z, _):
        for cut in range(0, rows, width):
            turned[pl.ds(TILE + cut, width), :] = scan[z, :, pl.ds(cut, width)].T
        for j in range(count):
            out[j, z, :, :] = turned[pl.ds(first + j * own, tall), :]
        return 0

    lax.fori_loop(0, sections, section, 0)


def slice_kernel(field, gate_below, gate_above, low, high):
    del gate_below, gate_above
    blocks, sections = field.shape[:2]
    width = low.shape[1]

    def plane(z, _):
        for out, at in ((low, z), (high, z + sections - width)):
            for i in range(blocks):
                out[i, z, :, :] = field[i, at, :, :]
        return 0

    lax.fori_loop(0, width, plane, 0)


def plane_kernel(field, before, after, low, high):
    blocks, sections, rows, _ = field.shape
    width = low.shape[1]

    def plane(z, _):
        for out, at in ((low, z), (high, z + sections - width)):
            for i in range(blocks):
                out[i, z, pl.ds(0, SENT), :] = before[i, at, :, :]
                out[i, z, pl.ds(GAP, rows), :] = field[i, at, :, :]
                out[i, z, pl.ds(GAP + rows, SENT), :] = after[i, at, :, :]
        return 0

    lax.fori_loop(0, width, plane, 0)


def misfit_kernel(moved, fixed, sums, misfit, low_rows, high_rows, total_ref):
    blocks, sections, rows, _ = moved.shape

    def section(z, acc):
        for i in range(blocks):
            for r in range(0, rows, TILE):
                value = moved[i, z, pl.ds(r, TILE), :] - fixed[i, z, pl.ds(r, TILE), :]
                misfit[i, z, pl.ds(r, TILE), :] = value
                acc = acc + value * value
                if r == 0:
                    low_rows[i, z, :, :] = value[:SENT]
                if r == rows - TILE:
                    high_rows[i, z, :, :] = value[TILE - SENT :]
        return acc

    zero = jnp.zeros((TILE, LANES), jnp.float32)
    total_ref[...] = 0.5 * (lax.fori_loop(0, sections, section, zero) + sums[...])


def pack_kernel(vel, sti, low_rows, high_rows, low, high, sem):
    _, sections, rows, _ = vel.shape
    copies = []
    for half, (out, at, one) in enumerate(((low, 0, 0), (high, sections - WIDE, sections - 1))):
        for c in range(3):
            copies.append(pltpu.make_async_copy(
                vel.at[c, pl.ds(at, WIDE)], out.at[pl.ds(c * WIDE, WIDE)], sem.at[4 * half + c]
            ))
        copies.append(pltpu.make_async_copy(
            sti.at[pl.ds(one, 1)], out.at[pl.ds(3 * WIDE, 1)], sem.at[4 * half + 3]
        ))
    for copy in copies:
        copy.start()
    for c in range(3):
        for z in range(sections):
            at = pl.ds((c * sections + z) * WIDE, WIDE)
            low_rows[at, :] = vel[c, z, pl.ds(0, WIDE), :]
            high_rows[at, :] = vel[c, z, pl.ds(rows - WIDE, WIDE), :]
    for z in range(sections):
        at = pl.ds(3 * sections * WIDE + z, 1)
        low_rows[at, :] = sti[z, pl.ds(0, 1), :]
        high_rows[at, :] = sti[z, pl.ds(rows - 1, 1), :]
    for copy in copies:
        copy.wait()


def corner_kernel(before, after, low, high):
    size = WIDE * WIDE
    sections = before.shape[0] // (3 * WIDE + 1)
    for c in range(3):
        for half, src in enumerate((before, after)):
            to = pl.ds((half * 3 + c) * size, size)
            low[to, :] = src[pl.ds(c * sections * WIDE, size), :]
            high[to, :] = src[pl.ds((c + 1) * sections * WIDE - size, size), :]


def groups(rows, reach):
    if reach == 0:
        return [GAP + g for g in range(0, rows, TILE)]
    return [1 + g for g in range(0, rows, TILE)] + [rows + 2 * GAP - 1 - TILE]


def masked(value, start, rows, flags):
    row = start + lax.broadcasted_iota(jnp.int32, value.shape, 0)
    if start < GAP:
        return jnp.where((row >= GAP) | (flags[2] > 0.5), value, 0.0)
    if start + TILE > GAP + rows:
        return jnp.where((row < GAP + rows) | (flags[3] > 0.5), value, 0.0)
    return value


def weights(flags, z, low, high):
    factor = jnp.where(z < low, flags[0], jnp.where(z >= high, flags[1], 1.0))
    return SELF * factor, WEIGHT * factor


def forward_kernel(flags, own, below, above, ext, moved_ref, kept, *scratch):
    levels, (vel, own_sem, vel_sem, kept_sem) = scratch[:STEPS], scratch[STEPS:]
    blocks, sections, rows, _ = moved_ref.shape
    first = [
        pltpu.make_async_copy(src, levels[0].at[:, pl.ds(at, src.shape[1])], own_sem.at[n])
        for n, (src, at) in enumerate(((below, 0), (own, STEPS), (above, STEPS + sections)))
    ]

    def load(z):
        return pltpu.make_async_copy(ext.at[:, :, z], vel.at[:, :, z], vel_sem.at[z])

    for copy in first:
        copy.start()
    for z in range(sections + 2 * WIDE):
        load(z).start()
    for copy in first:
        copy.wait()
    copies = []
    for step in range(STEPS):
        src = levels[step]
        if step > 0:
            copies.append(
                pltpu.make_async_copy(
                    src.at[:, pl.ds(STEPS - 1, sections + 2)], kept.at[step - 1], kept_sem.at[step - 1]
                )
            )
            copies[-1].start()
        reach = STEPS - 1 - step

        def plane(z, _, src=src, step=step, reach=reach):
            if step == 0:
                load(z - 1).wait()
            keep, weight = weights(flags, z, STEPS, STEPS + sections)
            for r in groups(rows, reach):
                here = pl.ds(r, TILE)
                mids = [src[i, z, here, :] for i in range(blocks)]
                plus, minus = edges_of(mids)
                for i in range(blocks):
                    zp, zm = src[i, z + 1, here, :], src[i, z - 1, here, :]
                    xp, xm = src[i, z, pl.ds(r + 1, TILE), :], src[i, z, pl.ds(r - 1, TILE), :]
                    yp, ym = plus[i], minus[i]
                    total = (zp + zm) - vel[0, i, z - 1, here, :] * (zp - zm)
                    total = total + ((xp + xm) - vel[1, i, z - 1, here, :] * (xp - xm))
                    total = total + ((yp + ym) - vel[2, i, z - 1, here, :] * (yp - ym))
                    value = keep * mids[i] + weight * total
                    if step == STEPS - 1:
                        moved_ref[i, z - STEPS, pl.ds(r - GAP, TILE), :] = value
                    else:
                        levels[step + 1][i, z, here, :] = masked(value, r, rows, flags)
            return 0

        lax.fori_loop(STEPS - reach, STEPS + sections + reach, plane, 0)
    for copy in copies:
        copy.wait()


def adjoint_kernel(flags, own, below, above, before, after, ext, start, start_below, start_above,
                   kept_all, reg_all, gate, grad_all, *scratch):
    del gate
    levels, (vel, kept, reg, grad_ref, vel_sem, kept_sem, reg_sem, grad_sem) = scratch[:STEPS], scratch[STEPS:]
    blocks, sections, rows, _ = own.shape

    def load(z):
        return pltpu.make_async_copy(ext.at[:, :, z], vel.at[:, :, z], vel_sem.at[z])

    def save(z):
        return pltpu.make_async_copy(grad_ref.at[:, z], grad_all.at[:, z], grad_sem.at[z])

    later = [
        pltpu.make_async_copy(src, kept.at[0, :, pl.ds(at, src.shape[1])], kept_sem.at[STEPS - 1 + n])
        for n, (src, at) in enumerate((
            (start_below.at[:, pl.ds(STEPS - 1, 1)], 0),
            (start, 1),
            (start_above.at[:, pl.ds(0, 1)], sections + 1),
        ))
    ] + [
        pltpu.make_async_copy(kept_all.at[k], kept.at[k + 1], kept_sem.at[k]) for k in range(STEPS - 1)
    ] + [pltpu.make_async_copy(reg_all, reg, reg_sem.at[0])]
    for z in range(sections + 2 * WIDE):
        load(z).start()
    for copy in later:
        copy.start()
    fill(levels[0], own, below, above, before, after, WIDE)
    load(0).wait()
    load(1).wait()
    for step in range(WIDE):
        src, out = levels[step], levels[step + 1]
        reach = WIDE - 1 - step

        def plane(z, _, src=src, out=out, reach=reach):
            if reach == WIDE - 1:
                load(z + 1).wait()
            keep, weight = weights(flags, z, WIDE, WIDE + sections)
            for r in groups(rows, reach):
                here, up, down = pl.ds(r, TILE), pl.ds(r + 1, TILE), pl.ds(r - 1, TILE)
                mids = [src[i, z, here, :] for i in range(blocks)]
                prods = [mids[i] * vel[2, i, z, here, :] for i in range(blocks)]
                plus, minus = edges(
                    [m + p for m, p in zip(mids, prods)], [m - p for m, p in zip(mids, prods)]
                )
                for i in range(blocks):
                    zp, zm = src[i, z + 1, here, :], src[i, z - 1, here, :]
                    xp, xm = src[i, z, up, :], src[i, z, down, :]
                    total = plus[i] + minus[i]
                    total = total + (zp + zp * vel[0, i, z + 1, here, :])
                    total = total + (zm - zm * vel[0, i, z - 1, here, :])
                    total = total + (xp + xp * vel[1, i, z, up, :])
                    total = total + (xm - xm * vel[1, i, z, down, :])
                    value = keep * mids[i] + weight * total
                    if reach > 0:
                        value = masked(value, r, rows, flags)
                    out[i, z, here, :] = value
            return 0

        lax.fori_loop(WIDE - reach, WIDE + sections + reach, plane, 0)

    for copy in later:
        copy.wait()

    def slope(z, _):
        for r in groups(rows, 0):
            here, up, down = pl.ds(r, TILE), pl.ds(r + 1, TILE), pl.ds(r - 1, TILE)
            at = pl.ds(r - GAP, TILE)
            sums = [[None] * 3 for _ in range(blocks)]
            for k in range(STEPS):
                adj = [levels[STEPS - 1 - k][i, z + WIDE, here, :] for i in range(blocks)]
                plus, minus = edges_of([kept[k, i, z + 1, here, :] for i in range(blocks)])
                for i in range(blocks):
                    parts = (
                        adj[i] * (kept[k, i, z + 2, here, :] - kept[k, i, z, here, :]),
                        adj[i] * (kept[k, i, z + 1, up, :] - kept[k, i, z + 1, down, :]),
                        adj[i] * (plus[i] - minus[i]),
                    )
                    for a in range(3):
                        sums[i][a] = parts[a] if k == 0 else sums[i][a] + parts[a]
            for i in range(blocks):
                lanes = pl.ds(i * LANES, LANES)
                for a in range(3):
                    grad_ref[a, z, at, lanes] = reg[a, z, at, lanes] - (0.5 * DT) * sums[i][a]
        save(z).start()
        return 0

    lax.fori_loop(0, sections, slope, 0)
    for z in range(sections):
        save(z).wait()


def lay(out, src, z):
    rows, width = src.shape
    for i in range(width // LANES):
        out[i, z, pl.ds(GAP, rows), :] = src[:, pl.ds(i * LANES, LANES)]


def lay_rows(out, z, row, src, at, count):
    for i in range(src.shape[1] // LANES):
        out[i, z, pl.ds(row, count), :] = src[pl.ds(at, count), pl.ds(i * LANES, LANES)]


def extend_kernel(vel, planes_below, planes_above, before, after, corners_below, corners_above, ext_ref):
    _, sections, rows, _ = vel.shape

    def mid(z, _):
        for c in range(3):
            lay(ext_ref.at[c], vel.at[c, z], z + WIDE)
        return 0

    def far(z, _):
        for c in range(3):
            lay(ext_ref.at[c], planes_below.at[c * WIDE + z], z)
            lay(ext_ref.at[c], planes_above.at[c * WIDE + z], z + WIDE + sections)
        return 0

    lax.fori_loop(0, sections, mid, 0)
    lax.fori_loop(0, WIDE, far, 0)
    low, high = GAP - WIDE, GAP + rows
    for c in range(3):
        for z in range(sections):
            at = (c * sections + z) * WIDE
            lay_rows(ext_ref.at[c], z + WIDE, low, before, at, WIDE)
            lay_rows(ext_ref.at[c], z + WIDE, high, after, at, WIDE)
        for z in range(WIDE):
            at, half = (c * WIDE + z) * WIDE, 3 * WIDE * WIDE
            for src, z_out in ((corners_below, z), (corners_above, z + WIDE + sections)):
                lay_rows(ext_ref.at[c], z_out, low, src, at, WIDE)
                lay_rows(ext_ref.at[c], z_out, high, src, at + half, WIDE)


def regular_kernel(gate, ext_ref, sti, planes_below, planes_above, before, after, reg_ref, sum_ref, sti_ext):
    del gate
    sections, rows, width = sti.shape
    blocks = width // LANES

    def mid(z, _):
        lay(sti_ext, sti.at[z], z + 1)
        return 0

    lax.fori_loop(0, sections, mid, 0)
    lay(sti_ext, planes_below.at[3 * WIDE], 0)
    lay(sti_ext, planes_above.at[3 * WIDE], sections + 1)
    for z in range(sections):
        at = 3 * sections * WIDE + z
        lay_rows(sti_ext, z + 1, GAP - 1, before, at, 1)
        lay_rows(sti_ext, z + 1, GAP + rows, after, at, 1)

    def plane(z, acc):
        for r in groups(rows, 0):
            here, up, down = pl.ds(r, TILE), pl.ds(r + 1, TILE), pl.ds(r - 1, TILE)
            at = pl.ds(r - GAP, TILE)
            s_mid = [sti_ext[i, z + 1, here, :] for i in range(blocks)]
            s_plus, s_minus = edges_of(s_mid)
            faces = []
            for i in range(blocks):
                s = s_mid[i]
                faces.append([
                    (s + sti_ext[i, z, here, :], s + sti_ext[i, z + 2, here, :]),
                    (s + sti_ext[i, z + 1, down, :], s + sti_ext[i, z + 1, up, :]),
                    (s + s_minus[i], s + s_plus[i]),
                ])
            for c in range(3):
                v_mid = [ext_ref[c, i, z + WIDE, here, :] for i in range(blocks)]
                v_plus, v_minus = edges_of(v_mid)
                for i in range(blocks):
                    v = v_mid[i]
                    pairs = (
                        (ext_ref[c, i, z + WIDE - 1, here, :], ext_ref[c, i, z + WIDE + 1, here, :]),
                        (ext_ref[c, i, z + WIDE, down, :], ext_ref[c, i, z + WIDE, up, :]),
                        (v_minus[i], v_plus[i]),
                    )
                    total = None
                    for (low, high), (f_low, f_high) in zip(pairs, faces[i]):
                        part = f_low * (v - low) + f_high * (v - high)
                        total = part if total is None else total + part
                    term = (0.5 * BETA) * total
                    reg_ref[c, z, at, pl.ds(i * LANES, LANES)] = term
                    acc = acc + v * term
        return acc

    acc = lax.fori_loop(0, sections, plane, jnp.zeros((TILE, LANES), jnp.float32))
    sum_ref[...] = acc


def after(value, *gates):
    def kernel(*refs):
        del refs

    return pl.pallas_call(
        kernel,
        out_shape=jax.ShapeDtypeStruct(value.shape, value.dtype),
        in_specs=[ANY] * (1 + len(gates)),
        out_specs=ANY,
        input_output_aliases={0: 0},
    )(value, *gates)


def to_blocks(scan, extra, gate):
    count = lax.axis_size("row")
    sections, width, rows = scan.shape
    own = rows // count
    tall = own + 2 * extra
    if width == LANES and rows % width == 0:
        return call(
            block_kernel, [(count, sections, tall, width)], [VMEM, ANY], [(rows + 2 * TILE, width)]
        )(scan, gate)[0]
    turned = jnp.pad(jnp.swapaxes(scan, 1, 2), ((0, 0), (extra, extra), (0, 0)))
    return jnp.stack([turned[:, j * own : j * own + tall] for j in range(count)])


def to_rows(parts):
    parts = lax.all_to_all(parts, "row", split_axis=0, concat_axis=0, tiled=True)
    count, sections, own, width = parts.shape
    if width == LANES:
        return parts
    whole = parts.transpose(1, 2, 0, 3).reshape(sections, own, count * width // LANES, LANES)
    return whole.transpose(2, 0, 1, 3)


def summed(part, axis, lows):
    count = lax.axis_size(axis)
    got = [lax.ppermute(part, axis, [(i, i ^ low) for i in range(count)]) for low in lows]
    if len(got) == 3:
        place = lax.axis_index(axis) // lows[0] % 4
        pairs = (part + got[0], got[1] + got[2])
        return jnp.where(place < 2, pairs[0], pairs[1]) + jnp.where(place < 2, pairs[1], pairs[0])
    return part + got[0]


def stages(axis):
    count, near, found = lax.axis_size(axis), 1, []
    while near < count:
        if count % (4 * near) == 0:
            found.append((axis, (near, 2 * near, 3 * near)))
            near *= 4
        else:
            found.append((axis, (near,)))
            near *= 2
    return found


def call(kernel, shapes, ins, scratch=(), outs=None, flops=0):
    return pl.pallas_call(
        kernel,
        out_shape=[jax.ShapeDtypeStruct(shape, jnp.float32) for shape in shapes],
        in_specs=ins,
        out_specs=outs or [VMEM] * len(shapes),
        scratch_shapes=[
            pltpu.VMEM(shape, jnp.float32) if isinstance(shape, tuple) else pltpu.SemaphoreType.DMA((shape,))
            for shape in scratch
        ],
        compiler_params=pltpu.CompilerParams(vmem_limit_bytes=63 << 20),
        cost_estimate=pl.CostEstimate(flops=flops, bytes_accessed=4 << 20, transcendentals=0),
    )


def local(template_scan, reference_scan, velocity, stiffness):
    _, sections, rows, width = velocity.shape
    blocks = width // LANES
    tall, deep = rows + 2 * GAP, sections + 2 * WIDE
    own = (blocks, sections, rows, LANES)
    ends = (blocks, sections, SENT, LANES)
    sec, row = lax.axis_index("sec"), lax.axis_index("row")
    flags = jnp.stack([
        sec > 0, sec < lax.axis_size("sec") - 1, row > 0, row < lax.axis_size("row") - 1
    ]).astype(jnp.float32)

    lines = (3 * WIDE + 1) * sections
    low_rows, high_rows, low, high = call(
        pack_kernel,
        [(lines, width)] * 2 + [(3 * WIDE + 1, rows, width)] * 2,
        [VMEM] * 2,
        [8],
        [VMEM] * 2 + [ANY] * 2,
    )(velocity, stiffness)
    before, after_ = exchange(low_rows, high_rows, "row")
    template = to_rows(to_blocks(template_scan, SENT, low_rows))
    below, above = exchange(low, high, "sec")
    corners = call(corner_kernel, [(6 * WIDE * WIDE, width)] * 2, [VMEM] * 2)(before, after_)
    (extended,) = call(extend_kernel, [(3, blocks, deep, tall, LANES)], [VMEM] * 7)(
        velocity, below, above, before, after_, *exchange(*corners, "sec")
    )

    fixed_blocks = to_blocks(reference_scan, 0, corners[0])
    low, high = call(slice_kernel, [(blocks, STEPS, tall, LANES)] * 2, [VMEM, ANY, ANY])(
        template, below, above
    )
    start = (template,) + exchange(low, high, "sec")
    fixed = to_rows(after(fixed_blocks, low))
    level = (blocks, sections + 2 * STEPS, tall, LANES)
    moved, kept = call(
        forward_kernel,
        [own, (STEPS - 1, blocks, sections + 2, tall, LANES)],
        [SMEM] + [ANY] * 4,
        [level] * STEPS + [(3, blocks, deep, tall, LANES), 3, deep, STEPS - 1],
        [VMEM, ANY],
        20 << 20,
    )(flags, *start, extended)

    reg, reg_sums = call(
        regular_kernel,
        [velocity.shape, (TILE, LANES)],
        [ANY] + [VMEM] * 6,
        [(blocks, sections + 2, tall, LANES)],
        flops=20 << 20,
    )(moved, extended, stiffness, below, above, before, after_)

    misfit, low_rows, high_rows, partial = call(misfit_kernel, [own, ends, ends, (TILE, LANES)], [VMEM] * 3)(
        moved, fixed, reg_sums
    )
    before, after_ = exchange(low_rows, high_rows, "row")
    low, high = call(plane_kernel, [(blocks, WIDE, tall, LANES)] * 2, [VMEM] * 3)(misfit, before, after_)
    below, above = exchange(low, high, "sec")
    along = stages("row")
    partial = after(summed(partial, *along[0]), low)
    for stage in along[1:]:
        partial = summed(partial, *stage)
    partial = after(partial, below, above)
    (gradient,) = call(
        adjoint_kernel,
        [velocity.shape],
        [SMEM] + [VMEM] * 5 + [ANY] * 7,
        [(blocks, deep, tall, LANES)] * STEPS
        + [(3, blocks, deep, tall, LANES), (STEPS, blocks, sections + 2, tall, LANES)]
        + [velocity.shape] * 2 + [deep, STEPS + 2, 1, sections],
        [ANY],
        20 << 20,
    )(flags, misfit, below, above, before, after_, extended, *start, kept, reg, partial)
    for stage in stages("sec"):
        partial = summed(partial, *stage)

    voxels = sections * rows * width * lax.axis_size("sec") * lax.axis_size("row")
    objective = jnp.sum(partial) / voxels
    return (gradient, objective)


def solution(mesh):
    return jax.shard_map(
        local,
        mesh=mesh,
        in_specs=(
            P("sec", "row", None),
            P("sec", "row", None),
            P(None, "sec", "row", None),
            P("sec", "row", None),
        ),
        out_specs=(P(None, "sec", "row", None), P()),
        check_vma=False,
    )
```

```python
import jax
import jax.numpy as jnp
from jax import lax
from jax.experimental import pallas as pl
from jax.experimental.pallas import tpu as pltpu
from jax.sharding import PartitionSpec as P

STEPS = 4

DT = 0.25
KAPPA = 0.5
BETA = 0.5

LANES = 128
TILE = 8
GAP = 4
SENT = 4
WIDE = STEPS - 1
WEIGHT = DT * KAPPA
SELF = 1.0 - 6.0 * WEIGHT
assert WEIGHT == DT * 0.5

VMEM = pl.BlockSpec(memory_space=pltpu.VMEM)
SMEM = pl.BlockSpec(memory_space=pltpu.SMEM)
ANY = pl.BlockSpec(memory_space=pl.ANY)


def exchange(low_part, high_part, axis):
    count = lax.axis_size(axis)
    below = lax.ppermute(high_part, axis, [(i, i + 1) for i in range(count - 1)])
    above = lax.ppermute(low_part, axis, [(i + 1, i) for i in range(count - 1)])
    return below, above


def edges(tiles_up, tiles_down):
    lane = lax.broadcasted_iota(jnp.int32, tiles_up[0].shape, 1)
    zero = jnp.zeros_like(tiles_up[0])
    up = [pltpu.roll(t, LANES - 1, 1) for t in tiles_up]
    down = [pltpu.roll(t, 1, 1) for t in tiles_down]
    plus = [jnp.where(lane == LANES - 1, n, u) for u, n in zip(up, up[1:] + [zero])]
    minus = [jnp.where(lane == 0, p, d) for d, p in zip(down, [zero] + down[:-1])]
    return plus, minus


def edges_of(tiles):
    return edges(tiles, tiles)


def fill(out, own, below, above, before, after, width):
    blocks, sections, rows, _ = own.shape

    def whole(z, _):
        for i in range(blocks):
            out[i, z + width, pl.ds(GAP, rows), :] = own[i, z, :, :]
            out[i, z + width, pl.ds(0, SENT), :] = before[i, z, :, :]
            out[i, z + width, pl.ds(GAP + rows, SENT), :] = after[i, z, :, :]
        return 0

    def halo(z, _):
        for planes, at in ((below, z), (above, z + width + sections)):
            for i in range(blocks):
                out[i, at, :, :] = planes[i, z, :, :]
        return 0

    lax.fori_loop(0, sections, whole, 0)
    lax.fori_loop(0, width, halo, 0)


def block_kernel(scan, gate, out, turned):
    del gate
    sections, width, rows = scan.shape
    count, _, tall, _ = out.shape
    own = rows // count
    first = TILE - (tall - own) // 2
    zero = jnp.zeros((TILE, width), jnp.float32)
    turned[pl.ds(0, TILE), :] = zero
    turned[pl.ds(TILE + rows, TILE), :] = zero

    def section(z, _):
        for cut in range(0, rows, width):
            turned[pl.ds(TILE + cut, width), :] = scan[z, :, pl.ds(cut, width)].T
        for j in range(count):
            out[j, z, :, :] = turned[pl.ds(first + j * own, tall), :]
        return 0

    lax.fori_loop(0, sections, section, 0)


def slice_kernel(field, gate_below, gate_above, low, high):
    del gate_below, gate_above
    blocks, sections = field.shape[:2]
    width = low.shape[1]

    def plane(z, _):
        for out, at in ((low, z), (high, z + sections - width)):
            for i in range(blocks):
                out[i, z, :, :] = field[i, at, :, :]
        return 0

    lax.fori_loop(0, width, plane, 0)


def plane_kernel(field, before, after, low, high):
    blocks, sections, rows, _ = field.shape
    width = low.shape[1]

    def plane(z, _):
        for out, at in ((low, z), (high, z + sections - width)):
            for i in range(blocks):
                out[i, z, pl.ds(0, SENT), :] = before[i, at, :, :]
                out[i, z, pl.ds(GAP, rows), :] = field[i, at, :, :]
                out[i, z, pl.ds(GAP + rows, SENT), :] = after[i, at, :, :]
        return 0

    lax.fori_loop(0, width, plane, 0)


def misfit_kernel(moved, fixed, sums, misfit, low_rows, high_rows, total_ref):
    blocks, sections, rows, _ = moved.shape

    def section(z, acc):
        for i in range(blocks):
            for r in range(0, rows, TILE):
                value = moved[i, z, pl.ds(r, TILE), :] - fixed[i, z, pl.ds(r, TILE), :]
                misfit[i, z, pl.ds(r, TILE), :] = value
                acc = acc + value * value
                if r == 0:
                    low_rows[i, z, :, :] = value[:SENT]
                if r == rows - TILE:
                    high_rows[i, z, :, :] = value[TILE - SENT :]
        return acc

    zero = jnp.zeros((TILE, LANES), jnp.float32)
    total_ref[...] = 0.5 * (lax.fori_loop(0, sections, section, zero) + sums[...])


def pack_kernel(vel, sti, low_rows, high_rows, low, high, sem):
    _, sections, rows, _ = vel.shape
    copies = []
    for half, (out, at, one) in enumerate(((low, 0, 0), (high, sections - WIDE, sections - 1))):
        for c in range(3):
            copies.append(pltpu.make_async_copy(
                vel.at[c, pl.ds(at, WIDE)], out.at[pl.ds(c * WIDE, WIDE)], sem.at[4 * half + c]
            ))
        copies.append(pltpu.make_async_copy(
            sti.at[pl.ds(one, 1)], out.at[pl.ds(3 * WIDE, 1)], sem.at[4 * half + 3]
        ))
    for copy in copies:
        copy.start()
    for c in range(3):
        for z in range(sections):
            at = pl.ds((c * sections + z) * WIDE, WIDE)
            low_rows[at, :] = vel[c, z, pl.ds(0, WIDE), :]
            high_rows[at, :] = vel[c, z, pl.ds(rows - WIDE, WIDE), :]
    for z in range(sections):
        at = pl.ds(3 * sections * WIDE + z, 1)
        low_rows[at, :] = sti[z, pl.ds(0, 1), :]
        high_rows[at, :] = sti[z, pl.ds(rows - 1, 1), :]
    for copy in copies:
        copy.wait()


def corner_kernel(before, after, low, high):
    size = WIDE * WIDE
    sections = before.shape[0] // (3 * WIDE + 1)
    for c in range(3):
        for half, src in enumerate((before, after)):
            to = pl.ds((half * 3 + c) * size, size)
            low[to, :] = src[pl.ds(c * sections * WIDE, size), :]
            high[to, :] = src[pl.ds((c + 1) * sections * WIDE - size, size), :]


def groups(rows, reach):
    if reach == 0:
        return [GAP + g for g in range(0, rows, TILE)]
    return [1 + g for g in range(0, rows, TILE)] + [rows + 2 * GAP - 1 - TILE]


def masked(value, start, rows, flags):
    row = start + lax.broadcasted_iota(jnp.int32, value.shape, 0)
    if start < GAP:
        return jnp.where((row >= GAP) | (flags[2] > 0.5), value, 0.0)
    if start + TILE > GAP + rows:
        return jnp.where((row < GAP + rows) | (flags[3] > 0.5), value, 0.0)
    return value


def weights(flags, z, low, high):
    factor = jnp.where(z < low, flags[0], jnp.where(z >= high, flags[1], 1.0))
    return SELF * factor, WEIGHT * factor


def forward_kernel(flags, own, below, above, ext, moved_ref, kept, *scratch):
    levels, (vel, own_sem, vel_sem, kept_sem) = scratch[:STEPS], scratch[STEPS:]
    blocks, sections, rows, _ = moved_ref.shape
    first = [
        pltpu.make_async_copy(src, levels[0].at[:, pl.ds(at, src.shape[1])], own_sem.at[n])
        for n, (src, at) in enumerate(((below, 0), (own, STEPS), (above, STEPS + sections)))
    ]

    def load(z):
        return pltpu.make_async_copy(ext.at[:, :, z], vel.at[:, :, z], vel_sem.at[z])

    for copy in first:
        copy.start()
    for z in range(sections + 2 * WIDE):
        load(z).start()
    for copy in first:
        copy.wait()
    copies = []
    for step in range(STEPS):
        src = levels[step]
        if step > 0:
            copies.append(
                pltpu.make_async_copy(
                    src.at[:, pl.ds(STEPS - 1, sections + 2)], kept.at[step - 1], kept_sem.at[step - 1]
                )
            )
            copies[-1].start()
        reach = STEPS - 1 - step

        def plane(z, _, src=src, step=step, reach=reach):
            if step == 0:
                load(z - 1).wait()
            keep, weight = weights(flags, z, STEPS, STEPS + sections)
            for r in groups(rows, reach):
                here = pl.ds(r, TILE)
                mids = [src[i, z, here, :] for i in range(blocks)]
                plus, minus = edges_of(mids)
                for i in range(blocks):
                    zp, zm = src[i, z + 1, here, :], src[i, z - 1, here, :]
                    xp, xm = src[i, z, pl.ds(r + 1, TILE), :], src[i, z, pl.ds(r - 1, TILE), :]
                    yp, ym = plus[i], minus[i]
                    total = (zp + zm) - vel[0, i, z - 1, here, :] * (zp - zm)
                    total = total + ((xp + xm) - vel[1, i, z - 1, here, :] * (xp - xm))
                    total = total + ((yp + ym) - vel[2, i, z - 1, here, :] * (yp - ym))
                    value = keep * mids[i] + weight * total
                    if step == STEPS - 1:
                        moved_ref[i, z - STEPS, pl.ds(r - GAP, TILE), :] = value
                    else:
                        levels[step + 1][i, z, here, :] = masked(value, r, rows, flags)
            return 0

        lax.fori_loop(STEPS - reach, STEPS + sections + reach, plane, 0)
    for copy in copies:
        copy.wait()


def adjoint_kernel(flags, own, below, above, before, after, ext, start, start_below, start_above,
                   kept_all, reg_all, gate, grad_all, *scratch):
    del gate
    levels, (vel, kept, reg, grad_ref, vel_sem, kept_sem, reg_sem, grad_sem) = scratch[:STEPS], scratch[STEPS:]
    blocks, sections, rows, _ = own.shape

    def load(z):
        return pltpu.make_async_copy(ext.at[:, :, z], vel.at[:, :, z], vel_sem.at[z])

    def save(z):
        return pltpu.make_async_copy(grad_ref.at[:, z], grad_all.at[:, z], grad_sem.at[z])

    later = [
        pltpu.make_async_copy(src, kept.at[0, :, pl.ds(at, src.shape[1])], kept_sem.at[STEPS - 1 + n])
        for n, (src, at) in enumerate((
            (start_below.at[:, pl.ds(STEPS - 1, 1)], 0),
            (start, 1),
            (start_above.at[:, pl.ds(0, 1)], sections + 1),
        ))
    ] + [
        pltpu.make_async_copy(kept_all.at[k], kept.at[k + 1], kept_sem.at[k]) for k in range(STEPS - 1)
    ] + [pltpu.make_async_copy(reg_all, reg, reg_sem.at[0])]
    for z in range(sections + 2 * WIDE):
        load(z).start()
    for copy in later:
        copy.start()
    fill(levels[0], own, below, above, before, after, WIDE)
    load(0).wait()
    load(1).wait()
    for step in range(WIDE):
        src, out = levels[step], levels[step + 1]
        reach = WIDE - 1 - step

        def plane(z, _, src=src, out=out, reach=reach):
            if reach == WIDE - 1:
                load(z + 1).wait()
            keep, weight = weights(flags, z, WIDE, WIDE + sections)
            for r in groups(rows, reach):
                here, up, down = pl.ds(r, TILE), pl.ds(r + 1, TILE), pl.ds(r - 1, TILE)
                mids = [src[i, z, here, :] for i in range(blocks)]
                prods = [mids[i] * vel[2, i, z, here, :] for i in range(blocks)]
                plus, minus = edges(
                    [m + p for m, p in zip(mids, prods)], [m - p for m, p in zip(mids, prods)]
                )
                for i in range(blocks):
                    zp, zm = src[i, z + 1, here, :], src[i, z - 1, here, :]
                    xp, xm = src[i, z, up, :], src[i, z, down, :]
                    total = plus[i] + minus[i]
                    total = total + (zp + zp * vel[0, i, z + 1, here, :])
                    total = total + (zm - zm * vel[0, i, z - 1, here, :])
                    total = total + (xp + xp * vel[1, i, z, up, :])
                    total = total + (xm - xm * vel[1, i, z, down, :])
                    value = keep * mids[i] + weight * total
                    if reach > 0:
                        value = masked(value, r, rows, flags)
                    out[i, z, here, :] = value
            return 0

        lax.fori_loop(WIDE - reach, WIDE + sections + reach, plane, 0)

    for copy in later:
        copy.wait()

    def slope(z, _):
        for r in groups(rows, 0):
            here, up, down = pl.ds(r, TILE), pl.ds(r + 1, TILE), pl.ds(r - 1, TILE)
            at = pl.ds(r - GAP, TILE)
            sums = [[None] * 3 for _ in range(blocks)]
            for k in range(STEPS):
                adj = [levels[STEPS - 1 - k][i, z + WIDE, here, :] for i in range(blocks)]
                plus, minus = edges_of([kept[k, i, z + 1, here, :] for i in range(blocks)])
                for i in range(blocks):
                    parts = (
                        adj[i] * (kept[k, i, z + 2, here, :] - kept[k, i, z, here, :]),
                        adj[i] * (kept[k, i, z + 1, up, :] - kept[k, i, z + 1, down, :]),
                        adj[i] * (plus[i] - minus[i]),
                    )
                    for a in range(3):
                        sums[i][a] = parts[a] if k == 0 else sums[i][a] + parts[a]
            for i in range(blocks):
                lanes = pl.ds(i * LANES, LANES)
                for a in range(3):
                    grad_ref[a, z, at, lanes] = reg[a, z, at, lanes] - (0.5 * DT) * sums[i][a]
        save(z).start()
        return 0

    lax.fori_loop(0, sections, slope, 0)
    for z in range(sections):
        save(z).wait()


def lay(out, src, z):
    rows, width = src.shape
    for i in range(width // LANES):
        out[i, z, pl.ds(GAP, rows), :] = src[:, pl.ds(i * LANES, LANES)]


def lay_rows(out, z, row, src, at, count):
    for i in range(src.shape[1] // LANES):
        out[i, z, pl.ds(row, count), :] = src[pl.ds(at, count), pl.ds(i * LANES, LANES)]


def extend_kernel(vel, sti, planes_below, planes_above, before, after, corners_below, corners_above,
                  ext_out, reg_ref, sum_ref, ext_ref, sti_ext, sem):
    _, sections, rows, width = vel.shape
    blocks = width // LANES

    def mid(z, _):
        for c in range(3):
            lay(ext_ref.at[c], vel.at[c, z], z + WIDE)
        return 0

    def far(z, _):
        for c in range(3):
            lay(ext_ref.at[c], planes_below.at[c * WIDE + z], z)
            lay(ext_ref.at[c], planes_above.at[c * WIDE + z], z + WIDE + sections)
        return 0

    lax.fori_loop(0, sections, mid, 0)
    lax.fori_loop(0, WIDE, far, 0)
    low, high = GAP - WIDE, GAP + rows
    for c in range(3):
        for z in range(sections):
            at = (c * sections + z) * WIDE
            lay_rows(ext_ref.at[c], z + WIDE, low, before, at, WIDE)
            lay_rows(ext_ref.at[c], z + WIDE, high, after, at, WIDE)
        for z in range(WIDE):
            at, half = (c * WIDE + z) * WIDE, 3 * WIDE * WIDE
            for src, z_out in ((corners_below, z), (corners_above, z + WIDE + sections)):
                lay_rows(ext_ref.at[c], z_out, low, src, at, WIDE)
                lay_rows(ext_ref.at[c], z_out, high, src, at + half, WIDE)
    out = pltpu.make_async_copy(ext_ref, ext_out, sem.at[0])
    out.start()

    def mid_s(z, _):
        lay(sti_ext, sti.at[z], z + 1)
        return 0

    lax.fori_loop(0, sections, mid_s, 0)
    lay(sti_ext, planes_below.at[3 * WIDE], 0)
    lay(sti_ext, planes_above.at[3 * WIDE], sections + 1)
    for z in range(sections):
        at = 3 * sections * WIDE + z
        lay_rows(sti_ext, z + 1, GAP - 1, before, at, 1)
        lay_rows(sti_ext, z + 1, GAP + rows, after, at, 1)

    def plane(z, acc):
        for r in groups(rows, 0):
            here, up, down = pl.ds(r, TILE), pl.ds(r + 1, TILE), pl.ds(r - 1, TILE)
            at = pl.ds(r - GAP, TILE)
            s_mid = [sti_ext[i, z + 1, here, :] for i in range(blocks)]
            s_plus, s_minus = edges_of(s_mid)
            faces = []
            for i in range(blocks):
                s = s_mid[i]
                faces.append([
                    (s + sti_ext[i, z, here, :], s + sti_ext[i, z + 2, here, :]),
                    (s + sti_ext[i, z + 1, down, :], s + sti_ext[i, z + 1, up, :]),
                    (s + s_minus[i], s + s_plus[i]),
                ])
            for c in range(3):
                v_mid = [ext_ref[c, i, z + WIDE, here, :] for i in range(blocks)]
                v_plus, v_minus = edges_of(v_mid)
                for i in range(blocks):
                    v = v_mid[i]
                    pairs = (
                        (ext_ref[c, i, z + WIDE - 1, here, :], ext_ref[c, i, z + WIDE + 1, here, :]),
                        (ext_ref[c, i, z + WIDE, down, :], ext_ref[c, i, z + WIDE, up, :]),
                        (v_minus[i], v_plus[i]),
                    )
                    total = None
                    for (low, high), (f_low, f_high) in zip(pairs, faces[i]):
                        part = f_low * (v - low) + f_high * (v - high)
                        total = part if total is None else total + part
                    term = (0.5 * BETA) * total
                    reg_ref[c, z, at, pl.ds(i * LANES, LANES)] = term
                    acc = acc + v * term
        return acc

    acc = lax.fori_loop(0, sections, plane, jnp.zeros((TILE, LANES), jnp.float32))
    sum_ref[...] = acc
    out.wait()


def after(value, *gates):
    def kernel(*refs):
        del refs

    return pl.pallas_call(
        kernel,
        out_shape=jax.ShapeDtypeStruct(value.shape, value.dtype),
        in_specs=[ANY] * (1 + len(gates)),
        out_specs=ANY,
        input_output_aliases={0: 0},
    )(value, *gates)


def to_blocks(scan, extra, gate):
    count = lax.axis_size("row")
    sections, width, rows = scan.shape
    own = rows // count
    tall = own + 2 * extra
    if width == LANES and rows % width == 0:
        return call(
            block_kernel, [(count, sections, tall, width)], [VMEM, ANY], [(rows + 2 * TILE, width)]
        )(scan, gate)[0]
    turned = jnp.pad(jnp.swapaxes(scan, 1, 2), ((0, 0), (extra, extra), (0, 0)))
    return jnp.stack([turned[:, j * own : j * own + tall] for j in range(count)])


def to_rows(parts):
    parts = lax.all_to_all(parts, "row", split_axis=0, concat_axis=0, tiled=True)
    count, sections, own, width = parts.shape
    if width == LANES:
        return parts
    whole = parts.transpose(1, 2, 0, 3).reshape(sections, own, count * width // LANES, LANES)
    return whole.transpose(2, 0, 1, 3)


def summed(part, axis, lows):
    count = lax.axis_size(axis)
    got = [lax.ppermute(part, axis, [(i, i ^ low) for i in range(count)]) for low in lows]
    if len(got) == 3:
        place = lax.axis_index(axis) // lows[0] % 4
        pairs = (part + got[0], got[1] + got[2])
        return jnp.where(place < 2, pairs[0], pairs[1]) + jnp.where(place < 2, pairs[1], pairs[0])
    return part + got[0]


def stages(axis):
    count, near, found = lax.axis_size(axis), 1, []
    while near < count:
        if count % (4 * near) == 0:
            found.append((axis, (near, 2 * near, 3 * near)))
            near *= 4
        else:
            found.append((axis, (near,)))
            near *= 2
    return found


def call(kernel, shapes, ins, scratch=(), outs=None, flops=0):
    return pl.pallas_call(
        kernel,
        out_shape=[jax.ShapeDtypeStruct(shape, jnp.float32) for shape in shapes],
        in_specs=ins,
        out_specs=outs or [VMEM] * len(shapes),
        scratch_shapes=[
            pltpu.VMEM(shape, jnp.float32) if isinstance(shape, tuple) else pltpu.SemaphoreType.DMA((shape,))
            for shape in scratch
        ],
        compiler_params=pltpu.CompilerParams(vmem_limit_bytes=63 << 20),
        cost_estimate=pl.CostEstimate(flops=flops, bytes_accessed=4 << 20, transcendentals=0),
    )


def local(template_scan, reference_scan, velocity, stiffness):
    _, sections, rows, width = velocity.shape
    blocks = width // LANES
    tall, deep = rows + 2 * GAP, sections + 2 * WIDE
    own = (blocks, sections, rows, LANES)
    ends = (blocks, sections, SENT, LANES)
    sec, row = lax.axis_index("sec"), lax.axis_index("row")
    flags = jnp.stack([
        sec > 0, sec < lax.axis_size("sec") - 1, row > 0, row < lax.axis_size("row") - 1
    ]).astype(jnp.float32)

    lines = (3 * WIDE + 1) * sections
    low_rows, high_rows, low, high = call(
        pack_kernel,
        [(lines, width)] * 2 + [(3 * WIDE + 1, rows, width)] * 2,
        [VMEM] * 2,
        [8],
        [VMEM] * 2 + [ANY] * 2,
    )(velocity, stiffness)
    before, after_ = exchange(low_rows, high_rows, "row")
    template = to_rows(to_blocks(template_scan, SENT, low_rows))
    below, above = exchange(low, high, "sec")
    corners = call(corner_kernel, [(6 * WIDE * WIDE, width)] * 2, [VMEM] * 2)(before, after_)
    extended, reg, reg_sums = call(
        extend_kernel,
        [(3, blocks, deep, tall, LANES), velocity.shape, (TILE, LANES)],
        [VMEM] * 8,
        [(3, blocks, deep, tall, LANES), (blocks, sections + 2, tall, LANES), 1],
        [ANY, VMEM, VMEM],
        20 << 20,
    )(velocity, stiffness, below, above, before, after_, *exchange(*corners, "sec"))

    fixed_blocks = to_blocks(reference_scan, 0, corners[0])
    low, high = call(slice_kernel, [(blocks, STEPS, tall, LANES)] * 2, [VMEM, ANY, ANY])(
        template, below, above
    )
    start = (template,) + exchange(low, high, "sec")
    fixed = to_rows(after(fixed_blocks, low))
    level = (blocks, sections + 2 * STEPS, tall, LANES)
    moved, kept = call(
        forward_kernel,
        [own, (STEPS - 1, blocks, sections + 2, tall, LANES)],
        [SMEM] + [ANY] * 4,
        [level] * STEPS + [(3, blocks, deep, tall, LANES), 3, deep, STEPS - 1],
        [VMEM, ANY],
        20 << 20,
    )(flags, *start, extended)

    misfit, low_rows, high_rows, partial = call(misfit_kernel, [own, ends, ends, (TILE, LANES)], [VMEM] * 3)(
        moved, fixed, reg_sums
    )
    before, after_ = exchange(low_rows, high_rows, "row")
    low, high = call(plane_kernel, [(blocks, WIDE, tall, LANES)] * 2, [VMEM] * 3)(misfit, before, after_)
    below, above = exchange(low, high, "sec")
    along = stages("row")
    partial = after(summed(partial, *along[0]), low)
    for stage in along[1:]:
        partial = summed(partial, *stage)
    partial = after(partial, below, above)
    (gradient,) = call(
        adjoint_kernel,
        [velocity.shape],
        [SMEM] + [VMEM] * 5 + [ANY] * 7,
        [(blocks, deep, tall, LANES)] * STEPS
        + [(3, blocks, deep, tall, LANES), (STEPS, blocks, sections + 2, tall, LANES)]
        + [velocity.shape] * 2 + [deep, STEPS + 2, 1, sections],
        [ANY],
        20 << 20,
    )(flags, misfit, below, above, before, after_, extended, *start, kept, reg, partial)
    for stage in stages("sec"):
        partial = summed(partial, *stage)

    voxels = sections * rows * width * lax.axis_size("sec") * lax.axis_size("row")
    objective = jnp.sum(partial) / voxels
    return (gradient, objective)


def solution(mesh):
    return jax.shard_map(
        local,
        mesh=mesh,
        in_specs=(
            P("sec", "row", None),
            P("sec", "row", None),
            P(None, "sec", "row", None),
            P("sec", "row", None),
        ),
        out_specs=(P(None, "sec", "row", None), P()),
        check_vma=False,
    )
```

```python
import jax
import jax.numpy as jnp
from jax import lax
from jax.experimental import pallas as pl
from jax.experimental.pallas import tpu as pltpu
from jax.sharding import PartitionSpec as P

STEPS = 4

DT = 0.25
KAPPA = 0.5
BETA = 0.5

LANES = 128
TILE = 8
GAP = 4
SENT = 4
WIDE = STEPS - 1
WEIGHT = DT * KAPPA
SELF = 1.0 - 6.0 * WEIGHT
assert WEIGHT == DT * 0.5

VMEM = pl.BlockSpec(memory_space=pltpu.VMEM)
SMEM = pl.BlockSpec(memory_space=pltpu.SMEM)
ANY = pl.BlockSpec(memory_space=pl.ANY)


def exchange(low_part, high_part, axis):
    count = lax.axis_size(axis)
    below = lax.ppermute(high_part, axis, [(i, i + 1) for i in range(count - 1)])
    above = lax.ppermute(low_part, axis, [(i + 1, i) for i in range(count - 1)])
    return below, above


def edges(tiles_up, tiles_down):
    lane = lax.broadcasted_iota(jnp.int32, tiles_up[0].shape, 1)
    zero = jnp.zeros_like(tiles_up[0])
    up = [pltpu.roll(t, LANES - 1, 1) for t in tiles_up]
    down = [pltpu.roll(t, 1, 1) for t in tiles_down]
    plus = [jnp.where(lane == LANES - 1, n, u) for u, n in zip(up, up[1:] + [zero])]
    minus = [jnp.where(lane == 0, p, d) for d, p in zip(down, [zero] + down[:-1])]
    return plus, minus


def edges_of(tiles):
    return edges(tiles, tiles)


def fill(out, own, below, above, before, after, width):
    blocks, sections, rows, _ = own.shape

    def whole(z, _):
        for i in range(blocks):
            out[i, z + width, pl.ds(GAP, rows), :] = own[i, z, :, :]
            out[i, z + width, pl.ds(0, SENT), :] = before[i, z, :, :]
            out[i, z + width, pl.ds(GAP + rows, SENT), :] = after[i, z, :, :]
        return 0

    def halo(z, _):
        for planes, at in ((below, z), (above, z + width + sections)):
            for i in range(blocks):
                out[i, at, :, :] = planes[i, z, :, :]
        return 0

    lax.fori_loop(0, sections, whole, 0)
    lax.fori_loop(0, width, halo, 0)


def block_kernel(scan, gate, out, turned):
    del gate
    sections, width, rows = scan.shape
    count, _, tall, _ = out.shape
    own = rows // count
    first = TILE - (tall - own) // 2
    zero = jnp.zeros((TILE, width), jnp.float32)
    turned[pl.ds(0, TILE), :] = zero
    turned[pl.ds(TILE + rows, TILE), :] = zero

    def section(z, _):
        for cut in range(0, rows, width):
            turned[pl.ds(TILE + cut, width), :] = scan[z, :, pl.ds(cut, width)].T
        for j in range(count):
            out[j, z, :, :] = turned[pl.ds(first + j * own, tall), :]
        return 0

    lax.fori_loop(0, sections, section, 0)


def slice_kernel(field, gate_below, gate_above, low, high):
    del gate_below, gate_above
    blocks, sections = field.shape[:2]
    width = low.shape[1]

    def plane(z, _):
        for out, at in ((low, z), (high, z + sections - width)):
            for i in range(blocks):
                out[i, z, :, :] = field[i, at, :, :]
        return 0

    lax.fori_loop(0, width, plane, 0)


def plane_kernel(field, before, after, low, high):
    blocks, sections, rows, _ = field.shape
    width = low.shape[1]

    def plane(z, _):
        for out, at in ((low, z), (high, z + sections - width)):
            for i in range(blocks):
                out[i, z, pl.ds(0, SENT), :] = before[i, at, :, :]
                out[i, z, pl.ds(GAP, rows), :] = field[i, at, :, :]
                out[i, z, pl.ds(GAP + rows, SENT), :] = after[i, at, :, :]
        return 0

    lax.fori_loop(0, width, plane, 0)


def misfit_kernel(moved, fixed, sums, misfit, low_rows, high_rows, total_ref):
    blocks, sections, rows, _ = moved.shape

    def section(z, acc):
        for i in range(blocks):
            for r in range(0, rows, TILE):
                value = moved[i, z, pl.ds(r, TILE), :] - fixed[i, z, pl.ds(r, TILE), :]
                misfit[i, z, pl.ds(r, TILE), :] = value
                acc = acc + value * value
                if r == 0:
                    low_rows[i, z, :, :] = value[:SENT]
                if r == rows - TILE:
                    high_rows[i, z, :, :] = value[TILE - SENT :]
        return acc

    zero = jnp.zeros((TILE, LANES), jnp.float32)
    total_ref[...] = 0.5 * (lax.fori_loop(0, sections, section, zero) + sums[...])


def pack_kernel(vel, sti, low_rows, high_rows, low, high, sem):
    _, sections, rows, _ = vel.shape
    copies = []
    for half, (out, at, one) in enumerate(((low, 0, 0), (high, sections - WIDE, sections - 1))):
        for c in range(3):
            copies.append(pltpu.make_async_copy(
                vel.at[c, pl.ds(at, WIDE)], out.at[pl.ds(c * WIDE, WIDE)], sem.at[4 * half + c]
            ))
        copies.append(pltpu.make_async_copy(
            sti.at[pl.ds(one, 1)], out.at[pl.ds(3 * WIDE, 1)], sem.at[4 * half + 3]
        ))
    for copy in copies:
        copy.start()
    for c in range(3):
        for z in range(sections):
            at = pl.ds((c * sections + z) * WIDE, WIDE)
            low_rows[at, :] = vel[c, z, pl.ds(0, WIDE), :]
            high_rows[at, :] = vel[c, z, pl.ds(rows - WIDE, WIDE), :]
    for z in range(sections):
        at = pl.ds(3 * sections * WIDE + z, 1)
        low_rows[at, :] = sti[z, pl.ds(0, 1), :]
        high_rows[at, :] = sti[z, pl.ds(rows - 1, 1), :]
    for copy in copies:
        copy.wait()


def corner_kernel(before, after, low, high):
    size = WIDE * WIDE
    sections = before.shape[0] // (3 * WIDE + 1)
    for c in range(3):
        for half, src in enumerate((before, after)):
            to = pl.ds((half * 3 + c) * size, size)
            low[to, :] = src[pl.ds(c * sections * WIDE, size), :]
            high[to, :] = src[pl.ds((c + 1) * sections * WIDE - size, size), :]


def groups(rows, reach):
    if reach == 0:
        return [GAP + g for g in range(0, rows, TILE)]
    return [1 + g for g in range(0, rows, TILE)] + [rows + 2 * GAP - 1 - TILE]


def masked(value, start, rows, flags):
    row = start + lax.broadcasted_iota(jnp.int32, value.shape, 0)
    if start < GAP:
        return jnp.where((row >= GAP) | (flags[2] > 0.5), value, 0.0)
    if start + TILE > GAP + rows:
        return jnp.where((row < GAP + rows) | (flags[3] > 0.5), value, 0.0)
    return value


def weights(flags, z, low, high):
    factor = jnp.where(z < low, flags[0], jnp.where(z >= high, flags[1], 1.0))
    return SELF * factor, WEIGHT * factor


def forward_kernel(flags, own, below, above, ext, moved_ref, kept, *scratch):
    levels, (vel, own_sem, vel_sem, kept_sem) = scratch[:STEPS], scratch[STEPS:]
    blocks, sections, rows, _ = moved_ref.shape
    first = [
        pltpu.make_async_copy(src, levels[0].at[:, pl.ds(at, src.shape[1])], own_sem.at[n])
        for n, (src, at) in enumerate(((below, 0), (own, STEPS), (above, STEPS + sections)))
    ]

    def load(z):
        return pltpu.make_async_copy(ext.at[:, :, z], vel.at[:, :, z], vel_sem.at[z])

    for copy in first:
        copy.start()
    for z in range(sections + 2 * WIDE):
        load(z).start()
    for copy in first:
        copy.wait()
    copies = []
    for step in range(STEPS):
        src = levels[step]
        if step > 0:
            copies.append(
                pltpu.make_async_copy(
                    src.at[:, pl.ds(STEPS - 1, sections + 2)], kept.at[step - 1], kept_sem.at[step - 1]
                )
            )
            copies[-1].start()
        reach = STEPS - 1 - step

        def plane(z, _, src=src, step=step, reach=reach):
            if step == 0:
                load(z - 1).wait()
            keep, weight = weights(flags, z, STEPS, STEPS + sections)
            for r in groups(rows, reach):
                here = pl.ds(r, TILE)
                mids = [src[i, z, here, :] for i in range(blocks)]
                plus, minus = edges_of(mids)
                for i in range(blocks):
                    zp, zm = src[i, z + 1, here, :], src[i, z - 1, here, :]
                    xp, xm = src[i, z, pl.ds(r + 1, TILE), :], src[i, z, pl.ds(r - 1, TILE), :]
                    yp, ym = plus[i], minus[i]
                    total = (zp + zm) - vel[0, i, z - 1, here, :] * (zp - zm)
                    total = total + ((xp + xm) - vel[1, i, z - 1, here, :] * (xp - xm))
                    total = total + ((yp + ym) - vel[2, i, z - 1, here, :] * (yp - ym))
                    value = keep * mids[i] + weight * total
                    if step == STEPS - 1:
                        moved_ref[i, z - STEPS, pl.ds(r - GAP, TILE), :] = value
                    else:
                        levels[step + 1][i, z, here, :] = masked(value, r, rows, flags)
            return 0

        lax.fori_loop(STEPS - reach, STEPS + sections + reach, plane, 0)
    for copy in copies:
        copy.wait()


def adjoint_kernel(flags, own, below, above, before, after, ext, start, start_below, start_above,
                   kept_all, reg_all, gate, grad_all, *scratch):
    del gate
    levels, (vel, kept, reg, grad_ref, vel_sem, kept_sem, reg_sem, grad_sem) = scratch[:STEPS], scratch[STEPS:]
    blocks, sections, rows, _ = own.shape

    def load(z):
        return pltpu.make_async_copy(ext.at[:, :, z], vel.at[:, :, z], vel_sem.at[z])

    def save(z):
        return pltpu.make_async_copy(grad_ref.at[:, z], grad_all.at[:, z], grad_sem.at[z])

    later = [
        pltpu.make_async_copy(src, kept.at[0, :, pl.ds(at, src.shape[1])], kept_sem.at[STEPS - 1 + n])
        for n, (src, at) in enumerate((
            (start_below.at[:, pl.ds(STEPS - 1, 1)], 0),
            (start, 1),
            (start_above.at[:, pl.ds(0, 1)], sections + 1),
        ))
    ] + [
        pltpu.make_async_copy(kept_all.at[k], kept.at[k + 1], kept_sem.at[k]) for k in range(STEPS - 1)
    ] + [pltpu.make_async_copy(reg_all, reg, reg_sem.at[0])]
    for z in range(sections + 2 * WIDE):
        load(z).start()
    for copy in later:
        copy.start()
    fill(levels[0], own, below, above, before, after, WIDE)
    load(0).wait()
    load(1).wait()
    for step in range(WIDE):
        src, out = levels[step], levels[step + 1]
        reach = WIDE - 1 - step

        def plane(z, _, src=src, out=out, reach=reach):
            if reach == WIDE - 1:
                load(z + 1).wait()
            keep, weight = weights(flags, z, WIDE, WIDE + sections)
            for r in groups(rows, reach):
                here, up, down = pl.ds(r, TILE), pl.ds(r + 1, TILE), pl.ds(r - 1, TILE)
                mids = [src[i, z, here, :] for i in range(blocks)]
                prods = [mids[i] * vel[2, i, z, here, :] for i in range(blocks)]
                plus, minus = edges(
                    [m + p for m, p in zip(mids, prods)], [m - p for m, p in zip(mids, prods)]
                )
                for i in range(blocks):
                    zp, zm = src[i, z + 1, here, :], src[i, z - 1, here, :]
                    xp, xm = src[i, z, up, :], src[i, z, down, :]
                    total = plus[i] + minus[i]
                    total = total + (zp + zp * vel[0, i, z + 1, here, :])
                    total = total + (zm - zm * vel[0, i, z - 1, here, :])
                    total = total + (xp + xp * vel[1, i, z, up, :])
                    total = total + (xm - xm * vel[1, i, z, down, :])
                    value = keep * mids[i] + weight * total
                    if reach > 0:
                        value = masked(value, r, rows, flags)
                    out[i, z, here, :] = value
            return 0

        lax.fori_loop(WIDE - reach, WIDE + sections + reach, plane, 0)

    for copy in later:
        copy.wait()

    def slope(z, _):
        for r in groups(rows, 0):
            here, up, down = pl.ds(r, TILE), pl.ds(r + 1, TILE), pl.ds(r - 1, TILE)
            at = pl.ds(r - GAP, TILE)
            sums = [[None] * 3 for _ in range(blocks)]
            for k in range(STEPS):
                adj = [levels[STEPS - 1 - k][i, z + WIDE, here, :] for i in range(blocks)]
                plus, minus = edges_of([kept[k, i, z + 1, here, :] for i in range(blocks)])
                for i in range(blocks):
                    parts = (
                        adj[i] * (kept[k, i, z + 2, here, :] - kept[k, i, z, here, :]),
                        adj[i] * (kept[k, i, z + 1, up, :] - kept[k, i, z + 1, down, :]),
                        adj[i] * (plus[i] - minus[i]),
                    )
                    for a in range(3):
                        sums[i][a] = parts[a] if k == 0 else sums[i][a] + parts[a]
            for i in range(blocks):
                lanes = pl.ds(i * LANES, LANES)
                for a in range(3):
                    grad_ref[a, z, at, lanes] = reg[a, z, at, lanes] - (0.5 * DT) * sums[i][a]
        save(z).start()
        return 0

    lax.fori_loop(0, sections, slope, 0)
    for z in range(sections):
        save(z).wait()


def lay(out, src, z):
    rows, width = src.shape
    for i in range(width // LANES):
        out[i, z, pl.ds(GAP, rows), :] = src[:, pl.ds(i * LANES, LANES)]


def lay_rows(out, z, row, src, at, count):
    for i in range(src.shape[1] // LANES):
        out[i, z, pl.ds(row, count), :] = src[pl.ds(at, count), pl.ds(i * LANES, LANES)]


def extend_kernel(vel, sti, planes_below, planes_above, before, after, corners_below, corners_above,
                  ext_out, reg_ref, sum_ref, ext_ref, sti_ext, sem):
    _, sections, rows, width = vel.shape
    blocks = width // LANES

    def mid(z, _):
        for c in range(3):
            lay(ext_ref.at[c], vel.at[c, z], z + WIDE)
        return 0

    def far(z, _):
        for c in range(3):
            lay(ext_ref.at[c], planes_below.at[c * WIDE + z], z)
            lay(ext_ref.at[c], planes_above.at[c * WIDE + z], z + WIDE + sections)
        return 0

    lax.fori_loop(0, sections, mid, 0)
    lax.fori_loop(0, WIDE, far, 0)
    low, high = GAP - WIDE, GAP + rows
    for c in range(3):
        for z in range(sections):
            at = (c * sections + z) * WIDE
            lay_rows(ext_ref.at[c], z + WIDE, low, before, at, WIDE)
            lay_rows(ext_ref.at[c], z + WIDE, high, after, at, WIDE)
        for z in range(WIDE):
            at, half = (c * WIDE + z) * WIDE, 3 * WIDE * WIDE
            for src, z_out in ((corners_below, z), (corners_above, z + WIDE + sections)):
                lay_rows(ext_ref.at[c], z_out, low, src, at, WIDE)
                lay_rows(ext_ref.at[c], z_out, high, src, at + half, WIDE)
    out = pltpu.make_async_copy(ext_ref, ext_out, sem.at[0])
    out.start()

    def mid_s(z, _):
        lay(sti_ext, sti.at[z], z + 1)
        return 0

    lax.fori_loop(0, sections, mid_s, 0)
    lay(sti_ext, planes_below.at[3 * WIDE], 0)
    lay(sti_ext, planes_above.at[3 * WIDE], sections + 1)
    for z in range(sections):
        at = 3 * sections * WIDE + z
        lay_rows(sti_ext, z + 1, GAP - 1, before, at, 1)
        lay_rows(sti_ext, z + 1, GAP + rows, after, at, 1)

    def plane(z, acc):
        for r in groups(rows, 0):
            here, up, down = pl.ds(r, TILE), pl.ds(r + 1, TILE), pl.ds(r - 1, TILE)
            at = pl.ds(r - GAP, TILE)
            s_mid = [sti_ext[i, z + 1, here, :] for i in range(blocks)]
            s_plus, s_minus = edges_of(s_mid)
            faces = []
            for i in range(blocks):
                s = s_mid[i]
                faces.append([
                    (s + sti_ext[i, z, here, :], s + sti_ext[i, z + 2, here, :]),
                    (s + sti_ext[i, z + 1, down, :], s + sti_ext[i, z + 1, up, :]),
                    (s + s_minus[i], s + s_plus[i]),
                ])
            for c in range(3):
                v_mid = [ext_ref[c, i, z + WIDE, here, :] for i in range(blocks)]
                v_plus, v_minus = edges_of(v_mid)
                for i in range(blocks):
                    v = v_mid[i]
                    pairs = (
                        (ext_ref[c, i, z + WIDE - 1, here, :], ext_ref[c, i, z + WIDE + 1, here, :]),
                        (ext_ref[c, i, z + WIDE, down, :], ext_ref[c, i, z + WIDE, up, :]),
                        (v_minus[i], v_plus[i]),
                    )
                    total = None
                    for (low, high), (f_low, f_high) in zip(pairs, faces[i]):
                        part = f_low * (v - low) + f_high * (v - high)
                        total = part if total is None else total + part
                    term = (0.5 * BETA) * total
                    reg_ref[c, z, at, pl.ds(i * LANES, LANES)] = term
                    acc = acc + v * term
        return acc

    acc = lax.fori_loop(0, sections, plane, jnp.zeros((TILE, LANES), jnp.float32))
    sum_ref[...] = acc
    out.wait()


def after(value, *gates):
    def kernel(*refs):
        del refs

    return pl.pallas_call(
        kernel,
        out_shape=jax.ShapeDtypeStruct(value.shape, value.dtype),
        in_specs=[ANY] * (1 + len(gates)),
        out_specs=ANY,
        input_output_aliases={0: 0},
    )(value, *gates)


def to_blocks(scan, extra, gate):
    count = lax.axis_size("row")
    sections, width, rows = scan.shape
    own = rows // count
    tall = own + 2 * extra
    if width == LANES and rows % width == 0:
        return call(
            block_kernel, [(count, sections, tall, width)], [VMEM, ANY], [(rows + 2 * TILE, width)]
        )(scan, gate)[0]
    turned = jnp.pad(jnp.swapaxes(scan, 1, 2), ((0, 0), (extra, extra), (0, 0)))
    return jnp.stack([turned[:, j * own : j * own + tall] for j in range(count)])


def to_rows(parts):
    parts = lax.all_to_all(parts, "row", split_axis=0, concat_axis=0, tiled=True)
    count, sections, own, width = parts.shape
    if width == LANES:
        return parts
    whole = parts.transpose(1, 2, 0, 3).reshape(sections, own, count * width // LANES, LANES)
    return whole.transpose(2, 0, 1, 3)


def summed(part, axis, lows):
    count = lax.axis_size(axis)
    got = [lax.ppermute(part, axis, [(i, i ^ low) for i in range(count)]) for low in lows]
    if len(got) == 3:
        place = lax.axis_index(axis) // lows[0] % 4
        pairs = (part + got[0], got[1] + got[2])
        return jnp.where(place < 2, pairs[0], pairs[1]) + jnp.where(place < 2, pairs[1], pairs[0])
    return part + got[0]


def stages(axis):
    count, near, found = lax.axis_size(axis), 1, []
    while near < count:
        if count % (4 * near) == 0:
            found.append((axis, (near, 2 * near, 3 * near)))
            near *= 4
        else:
            found.append((axis, (near,)))
            near *= 2
    return found


def call(kernel, shapes, ins, scratch=(), outs=None, flops=0):
    return pl.pallas_call(
        kernel,
        out_shape=[jax.ShapeDtypeStruct(shape, jnp.float32) for shape in shapes],
        in_specs=ins,
        out_specs=outs or [VMEM] * len(shapes),
        scratch_shapes=[
            pltpu.VMEM(shape, jnp.float32) if isinstance(shape, tuple) else pltpu.SemaphoreType.DMA((shape,))
            for shape in scratch
        ],
        compiler_params=pltpu.CompilerParams(vmem_limit_bytes=63 << 20),
        cost_estimate=pl.CostEstimate(flops=flops, bytes_accessed=4 << 20, transcendentals=0),
    )


def local(template_scan, reference_scan, velocity, stiffness):
    _, sections, rows, width = velocity.shape
    blocks = width // LANES
    tall, deep = rows + 2 * GAP, sections + 2 * WIDE
    own = (blocks, sections, rows, LANES)
    ends = (blocks, sections, SENT, LANES)
    sec, row = lax.axis_index("sec"), lax.axis_index("row")
    flags = jnp.stack([
        sec > 0, sec < lax.axis_size("sec") - 1, row > 0, row < lax.axis_size("row") - 1
    ]).astype(jnp.float32)

    lines = (3 * WIDE + 1) * sections
    low_rows, high_rows, low, high = call(
        pack_kernel,
        [(lines, width)] * 2 + [(3 * WIDE + 1, rows, width)] * 2,
        [VMEM] * 2,
        [8],
        [VMEM] * 2 + [ANY] * 2,
    )(velocity, stiffness)
    before, after_ = exchange(low_rows, high_rows, "row")
    template_blocks = to_blocks(template_scan, SENT, low_rows)
    template = to_rows(template_blocks)
    below, above = exchange(low, high, "sec")
    corners = call(corner_kernel, [(6 * WIDE * WIDE, width)] * 2, [VMEM] * 2)(before, after_)
    extended, reg, reg_sums = call(
        extend_kernel,
        [(3, blocks, deep, tall, LANES), velocity.shape, (TILE, LANES)],
        [VMEM] * 8,
        [(3, blocks, deep, tall, LANES), (blocks, sections + 2, tall, LANES), 1],
        [ANY, VMEM, VMEM],
        20 << 20,
    )(velocity, stiffness, below, above, before, after_, *exchange(*corners, "sec"))

    fixed_blocks = to_blocks(reference_scan, 0, template_blocks)
    low, high = call(slice_kernel, [(blocks, STEPS, tall, LANES)] * 2, [VMEM, ANY, ANY])(
        template, below, above
    )
    start = (template,) + exchange(low, high, "sec")
    fixed = to_rows(after(fixed_blocks, low))
    level = (blocks, sections + 2 * STEPS, tall, LANES)
    moved, kept = call(
        forward_kernel,
        [own, (STEPS - 1, blocks, sections + 2, tall, LANES)],
        [SMEM] + [ANY] * 4,
        [level] * STEPS + [(3, blocks, deep, tall, LANES), 3, deep, STEPS - 1],
        [VMEM, ANY],
        20 << 20,
    )(flags, *start, extended)

    misfit, low_rows, high_rows, partial = call(misfit_kernel, [own, ends, ends, (TILE, LANES)], [VMEM] * 3)(
        moved, fixed, reg_sums
    )
    before, after_ = exchange(low_rows, high_rows, "row")
    low, high = call(plane_kernel, [(blocks, WIDE, tall, LANES)] * 2, [VMEM] * 3)(misfit, before, after_)
    below, above = exchange(low, high, "sec")
    along = stages("row")
    partial = after(summed(partial, *along[0]), low)
    for stage in along[1:]:
        partial = summed(partial, *stage)
    partial = after(partial, below, above)
    (gradient,) = call(
        adjoint_kernel,
        [velocity.shape],
        [SMEM] + [VMEM] * 5 + [ANY] * 7,
        [(blocks, deep, tall, LANES)] * STEPS
        + [(3, blocks, deep, tall, LANES), (STEPS, blocks, sections + 2, tall, LANES)]
        + [velocity.shape] * 2 + [deep, STEPS + 2, 1, sections],
        [ANY],
        20 << 20,
    )(flags, misfit, below, above, before, after_, extended, *start, kept, reg, partial)
    for stage in stages("sec"):
        partial = summed(partial, *stage)

    voxels = sections * rows * width * lax.axis_size("sec") * lax.axis_size("row")
    objective = jnp.sum(partial) / voxels
    return (gradient, objective)


def solution(mesh):
    return jax.shard_map(
        local,
        mesh=mesh,
        in_specs=(
            P("sec", "row", None),
            P("sec", "row", None),
            P(None, "sec", "row", None),
            P("sec", "row", None),
        ),
        out_specs=(P(None, "sec", "row", None), P()),
        check_vma=False,
    )
```

```python
import jax
import jax.numpy as jnp
from jax import lax
from jax.experimental import pallas as pl
from jax.experimental.pallas import tpu as pltpu
from jax.sharding import PartitionSpec as P

STEPS = 4

DT = 0.25
KAPPA = 0.5
BETA = 0.5

LANES = 128
TILE = 8
GAP = 4
SENT = 4
WIDE = STEPS - 1
WEIGHT = DT * KAPPA
SELF = 1.0 - 6.0 * WEIGHT
assert WEIGHT == DT * 0.5

VMEM = pl.BlockSpec(memory_space=pltpu.VMEM)
SMEM = pl.BlockSpec(memory_space=pltpu.SMEM)
ANY = pl.BlockSpec(memory_space=pl.ANY)


def exchange(low_part, high_part, axis):
    count = lax.axis_size(axis)
    below = lax.ppermute(high_part, axis, [(i, i + 1) for i in range(count - 1)])
    above = lax.ppermute(low_part, axis, [(i + 1, i) for i in range(count - 1)])
    return below, above


def edges(tiles_up, tiles_down):
    lane = lax.broadcasted_iota(jnp.int32, tiles_up[0].shape, 1)
    zero = jnp.zeros_like(tiles_up[0])
    up = [pltpu.roll(t, LANES - 1, 1) for t in tiles_up]
    down = [pltpu.roll(t, 1, 1) for t in tiles_down]
    plus = [jnp.where(lane == LANES - 1, n, u) for u, n in zip(up, up[1:] + [zero])]
    minus = [jnp.where(lane == 0, p, d) for d, p in zip(down, [zero] + down[:-1])]
    return plus, minus


def edges_of(tiles):
    return edges(tiles, tiles)


def fill(out, own, below, above, before, after, width):
    blocks, sections, rows, _ = own.shape

    def whole(z, _):
        for i in range(blocks):
            out[i, z + width, pl.ds(GAP, rows), :] = own[i, z, :, :]
            out[i, z + width, pl.ds(0, SENT), :] = before[i, z, :, :]
            out[i, z + width, pl.ds(GAP + rows, SENT), :] = after[i, z, :, :]
        return 0

    def halo(z, _):
        for planes, at in ((below, z), (above, z + width + sections)):
            for i in range(blocks):
                out[i, at, :, :] = planes[i, z, :, :]
        return 0

    lax.fori_loop(0, sections, whole, 0)
    lax.fori_loop(0, width, halo, 0)


def block_kernel(scan, gate, out, turned):
    del gate
    sections, width, rows = scan.shape
    count, _, tall, _ = out.shape
    own = rows // count
    first = TILE - (tall - own) // 2
    zero = jnp.zeros((TILE, width), jnp.float32)
    turned[pl.ds(0, TILE), :] = zero
    turned[pl.ds(TILE + rows, TILE), :] = zero

    def section(z, _):
        for cut in range(0, rows, width):
            turned[pl.ds(TILE + cut, width), :] = scan[z, :, pl.ds(cut, width)].T
        for j in range(count):
            out[j, z, :, :] = turned[pl.ds(first + j * own, tall), :]
        return 0

    lax.fori_loop(0, sections, section, 0)


def slice_kernel(field, gate_below, gate_above, gate_corners, low, high):
    del gate_below, gate_above, gate_corners
    blocks, sections = field.shape[:2]
    width = low.shape[1]

    def plane(z, _):
        for out, at in ((low, z), (high, z + sections - width)):
            for i in range(blocks):
                out[i, z, :, :] = field[i, at, :, :]
        return 0

    lax.fori_loop(0, width, plane, 0)


def plane_kernel(field, before, after, low, high):
    blocks, sections, rows, _ = field.shape
    width = low.shape[1]

    def plane(z, _):
        for out, at in ((low, z), (high, z + sections - width)):
            for i in range(blocks):
                out[i, z, pl.ds(0, SENT), :] = before[i, at, :, :]
                out[i, z, pl.ds(GAP, rows), :] = field[i, at, :, :]
                out[i, z, pl.ds(GAP + rows, SENT), :] = after[i, at, :, :]
        return 0

    lax.fori_loop(0, width, plane, 0)


def misfit_kernel(moved, fixed, sums, misfit, low_rows, high_rows, total_ref):
    blocks, sections, rows, _ = moved.shape

    def section(z, acc):
        for i in range(blocks):
            for r in range(0, rows, TILE):
                value = moved[i, z, pl.ds(r, TILE), :] - fixed[i, z, pl.ds(r, TILE), :]
                misfit[i, z, pl.ds(r, TILE), :] = value
                acc = acc + value * value
                if r == 0:
                    low_rows[i, z, :, :] = value[:SENT]
                if r == rows - TILE:
                    high_rows[i, z, :, :] = value[TILE - SENT :]
        return acc

    zero = jnp.zeros((TILE, LANES), jnp.float32)
    total_ref[...] = 0.5 * (lax.fori_loop(0, sections, section, zero) + sums[...])


def pack_kernel(vel, sti, low_rows, high_rows, low, high, sem):
    _, sections, rows, _ = vel.shape
    copies = []
    for half, (out, at, one) in enumerate(((low, 0, 0), (high, sections - WIDE, sections - 1))):
        for c in range(3):
            copies.append(pltpu.make_async_copy(
                vel.at[c, pl.ds(at, WIDE)], out.at[pl.ds(c * WIDE, WIDE)], sem.at[4 * half + c]
            ))
        copies.append(pltpu.make_async_copy(
            sti.at[pl.ds(one, 1)], out.at[pl.ds(3 * WIDE, 1)], sem.at[4 * half + 3]
        ))
    for copy in copies:
        copy.start()
    for c in range(3):
        for z in range(sections):
            at = pl.ds((c * sections + z) * WIDE, WIDE)
            low_rows[at, :] = vel[c, z, pl.ds(0, WIDE), :]
            high_rows[at, :] = vel[c, z, pl.ds(rows - WIDE, WIDE), :]
    for z in range(sections):
        at = pl.ds(3 * sections * WIDE + z, 1)
        low_rows[at, :] = sti[z, pl.ds(0, 1), :]
        high_rows[at, :] = sti[z, pl.ds(rows - 1, 1), :]
    for copy in copies:
        copy.wait()


def corner_kernel(before, after, low, high):
    size = WIDE * WIDE
    sections = before.shape[0] // (3 * WIDE + 1)
    for c in range(3):
        for half, src in enumerate((before, after)):
            to = pl.ds((half * 3 + c) * size, size)
            low[to, :] = src[pl.ds(c * sections * WIDE, size), :]
            high[to, :] = src[pl.ds((c + 1) * sections * WIDE - size, size), :]


def groups(rows, reach):
    if reach == 0:
        return [GAP + g for g in range(0, rows, TILE)]
    return [1 + g for g in range(0, rows, TILE)] + [rows + 2 * GAP - 1 - TILE]


def masked(value, start, rows, flags):
    row = start + lax.broadcasted_iota(jnp.int32, value.shape, 0)
    if start < GAP:
        return jnp.where((row >= GAP) | (flags[2] > 0.5), value, 0.0)
    if start + TILE > GAP + rows:
        return jnp.where((row < GAP + rows) | (flags[3] > 0.5), value, 0.0)
    return value


def weights(flags, z, low, high):
    factor = jnp.where(z < low, flags[0], jnp.where(z >= high, flags[1], 1.0))
    return SELF * factor, WEIGHT * factor


def forward_kernel(flags, own, below, above, ext, moved_ref, kept, *scratch):
    levels, (vel, own_sem, vel_sem, kept_sem) = scratch[:STEPS], scratch[STEPS:]
    blocks, sections, rows, _ = moved_ref.shape
    first = [
        pltpu.make_async_copy(src, levels[0].at[:, pl.ds(at, src.shape[1])], own_sem.at[n])
        for n, (src, at) in enumerate(((below, 0), (own, STEPS), (above, STEPS + sections)))
    ]

    def load(z):
        return pltpu.make_async_copy(ext.at[:, :, z], vel.at[:, :, z], vel_sem.at[z])

    for copy in first:
        copy.start()
    for z in range(sections + 2 * WIDE):
        load(z).start()
    for copy in first:
        copy.wait()
    copies = []
    for step in range(STEPS):
        src = levels[step]
        if step > 0:
            copies.append(
                pltpu.make_async_copy(
                    src.at[:, pl.ds(STEPS - 1, sections + 2)], kept.at[step - 1], kept_sem.at[step - 1]
                )
            )
            copies[-1].start()
        reach = STEPS - 1 - step

        def plane(z, _, src=src, step=step, reach=reach):
            if step == 0:
                load(z - 1).wait()
            keep, weight = weights(flags, z, STEPS, STEPS + sections)
            for r in groups(rows, reach):
                here = pl.ds(r, TILE)
                mids = [src[i, z, here, :] for i in range(blocks)]
                plus, minus = edges_of(mids)
                for i in range(blocks):
                    zp, zm = src[i, z + 1, here, :], src[i, z - 1, here, :]
                    xp, xm = src[i, z, pl.ds(r + 1, TILE), :], src[i, z, pl.ds(r - 1, TILE), :]
                    yp, ym = plus[i], minus[i]
                    total = (zp + zm) - vel[0, i, z - 1, here, :] * (zp - zm)
                    total = total + ((xp + xm) - vel[1, i, z - 1, here, :] * (xp - xm))
                    total = total + ((yp + ym) - vel[2, i, z - 1, here, :] * (yp - ym))
                    value = keep * mids[i] + weight * total
                    if step == STEPS - 1:
                        moved_ref[i, z - STEPS, pl.ds(r - GAP, TILE), :] = value
                    else:
                        levels[step + 1][i, z, here, :] = masked(value, r, rows, flags)
            return 0

        lax.fori_loop(STEPS - reach, STEPS + sections + reach, plane, 0)
    for copy in copies:
        copy.wait()


def adjoint_kernel(flags, own, below, above, before, after, ext, start, start_below, start_above,
                   kept_all, reg_all, gate, grad_all, *scratch):
    del gate
    levels, (vel, kept, reg, grad_ref, vel_sem, kept_sem, reg_sem, grad_sem) = scratch[:STEPS], scratch[STEPS:]
    blocks, sections, rows, _ = own.shape

    def load(z):
        return pltpu.make_async_copy(ext.at[:, :, z], vel.at[:, :, z], vel_sem.at[z])

    def save(z):
        return pltpu.make_async_copy(grad_ref.at[:, z], grad_all.at[:, z], grad_sem.at[z])

    later = [
        pltpu.make_async_copy(src, kept.at[0, :, pl.ds(at, src.shape[1])], kept_sem.at[STEPS - 1 + n])
        for n, (src, at) in enumerate((
            (start_below.at[:, pl.ds(STEPS - 1, 1)], 0),
            (start, 1),
            (start_above.at[:, pl.ds(0, 1)], sections + 1),
        ))
    ] + [
        pltpu.make_async_copy(kept_all.at[k], kept.at[k + 1], kept_sem.at[k]) for k in range(STEPS - 1)
    ] + [pltpu.make_async_copy(reg_all, reg, reg_sem.at[0])]
    for z in range(sections + 2 * WIDE):
        load(z).start()
    for copy in later:
        copy.start()
    fill(levels[0], own, below, above, before, after, WIDE)
    load(0).wait()
    load(1).wait()
    for step in range(WIDE):
        src, out = levels[step], levels[step + 1]
        reach = WIDE - 1 - step

        def plane(z, _, src=src, out=out, reach=reach):
            if reach == WIDE - 1:
                load(z + 1).wait()
            keep, weight = weights(flags, z, WIDE, WIDE + sections)
            for r in groups(rows, reach):
                here, up, down = pl.ds(r, TILE), pl.ds(r + 1, TILE), pl.ds(r - 1, TILE)
                mids = [src[i, z, here, :] for i in range(blocks)]
                prods = [mids[i] * vel[2, i, z, here, :] for i in range(blocks)]
                plus, minus = edges(
                    [m + p for m, p in zip(mids, prods)], [m - p for m, p in zip(mids, prods)]
                )
                for i in range(blocks):
                    zp, zm = src[i, z + 1, here, :], src[i, z - 1, here, :]
                    xp, xm = src[i, z, up, :], src[i, z, down, :]
                    total = plus[i] + minus[i]
                    total = total + (zp + zp * vel[0, i, z + 1, here, :])
                    total = total + (zm - zm * vel[0, i, z - 1, here, :])
                    total = total + (xp + xp * vel[1, i, z, up, :])
                    total = total + (xm - xm * vel[1, i, z, down, :])
                    value = keep * mids[i] + weight * total
                    if reach > 0:
                        value = masked(value, r, rows, flags)
                    out[i, z, here, :] = value
            return 0

        lax.fori_loop(WIDE - reach, WIDE + sections + reach, plane, 0)

    for copy in later:
        copy.wait()

    def slope(z, _):
        for r in groups(rows, 0):
            here, up, down = pl.ds(r, TILE), pl.ds(r + 1, TILE), pl.ds(r - 1, TILE)
            at = pl.ds(r - GAP, TILE)
            sums = [[None] * 3 for _ in range(blocks)]
            for k in range(STEPS):
                adj = [levels[STEPS - 1 - k][i, z + WIDE, here, :] for i in range(blocks)]
                plus, minus = edges_of([kept[k, i, z + 1, here, :] for i in range(blocks)])
                for i in range(blocks):
                    parts = (
                        adj[i] * (kept[k, i, z + 2, here, :] - kept[k, i, z, here, :]),
                        adj[i] * (kept[k, i, z + 1, up, :] - kept[k, i, z + 1, down, :]),
                        adj[i] * (plus[i] - minus[i]),
                    )
                    for a in range(3):
                        sums[i][a] = parts[a] if k == 0 else sums[i][a] + parts[a]
            for i in range(blocks):
                lanes = pl.ds(i * LANES, LANES)
                for a in range(3):
                    grad_ref[a, z, at, lanes] = reg[a, z, at, lanes] - (0.5 * DT) * sums[i][a]
        save(z).start()
        return 0

    lax.fori_loop(0, sections, slope, 0)
    for z in range(sections):
        save(z).wait()


def lay(out, src, z):
    rows, width = src.shape
    for i in range(width // LANES):
        out[i, z, pl.ds(GAP, rows), :] = src[:, pl.ds(i * LANES, LANES)]


def lay_rows(out, z, row, src, at, count):
    for i in range(src.shape[1] // LANES):
        out[i, z, pl.ds(row, count), :] = src[pl.ds(at, count), pl.ds(i * LANES, LANES)]


def extend_kernel(vel, sti, planes_below, planes_above, before, after, corners_below, corners_above,
                  ext_out, reg_ref, sum_ref, ext_ref, sti_ext, sem):
    _, sections, rows, width = vel.shape
    blocks = width // LANES

    def mid(z, _):
        for c in range(3):
            lay(ext_ref.at[c], vel.at[c, z], z + WIDE)
        return 0

    def far(z, _):
        for c in range(3):
            lay(ext_ref.at[c], planes_below.at[c * WIDE + z], z)
            lay(ext_ref.at[c], planes_above.at[c * WIDE + z], z + WIDE + sections)
        return 0

    lax.fori_loop(0, sections, mid, 0)
    lax.fori_loop(0, WIDE, far, 0)
    low, high = GAP - WIDE, GAP + rows
    for c in range(3):
        for z in range(sections):
            at = (c * sections + z) * WIDE
            lay_rows(ext_ref.at[c], z + WIDE, low, before, at, WIDE)
            lay_rows(ext_ref.at[c], z + WIDE, high, after, at, WIDE)
        for z in range(WIDE):
            at, half = (c * WIDE + z) * WIDE, 3 * WIDE * WIDE
            for src, z_out in ((corners_below, z), (corners_above, z + WIDE + sections)):
                lay_rows(ext_ref.at[c], z_out, low, src, at, WIDE)
                lay_rows(ext_ref.at[c], z_out, high, src, at + half, WIDE)
    out = pltpu.make_async_copy(ext_ref, ext_out, sem.at[0])
    out.start()

    def mid_s(z, _):
        lay(sti_ext, sti.at[z], z + 1)
        return 0

    lax.fori_loop(0, sections, mid_s, 0)
    lay(sti_ext, planes_below.at[3 * WIDE], 0)
    lay(sti_ext, planes_above.at[3 * WIDE], sections + 1)
    for z in range(sections):
        at = 3 * sections * WIDE + z
        lay_rows(sti_ext, z + 1, GAP - 1, before, at, 1)
        lay_rows(sti_ext, z + 1, GAP + rows, after, at, 1)

    def plane(z, acc):
        for r in groups(rows, 0):
            here, up, down = pl.ds(r, TILE), pl.ds(r + 1, TILE), pl.ds(r - 1, TILE)
            at = pl.ds(r - GAP, TILE)
            s_mid = [sti_ext[i, z + 1, here, :] for i in range(blocks)]
            s_plus, s_minus = edges_of(s_mid)
            faces = []
            for i in range(blocks):
                s = s_mid[i]
                faces.append([
                    (s + sti_ext[i, z, here, :], s + sti_ext[i, z + 2, here, :]),
                    (s + sti_ext[i, z + 1, down, :], s + sti_ext[i, z + 1, up, :]),
                    (s + s_minus[i], s + s_plus[i]),
                ])
            for c in range(3):
                v_mid = [ext_ref[c, i, z + WIDE, here, :] for i in range(blocks)]
                v_plus, v_minus = edges_of(v_mid)
                for i in range(blocks):
                    v = v_mid[i]
                    pairs = (
                        (ext_ref[c, i, z + WIDE - 1, here, :], ext_ref[c, i, z + WIDE + 1, here, :]),
                        (ext_ref[c, i, z + WIDE, down, :], ext_ref[c, i, z + WIDE, up, :]),
                        (v_minus[i], v_plus[i]),
                    )
                    total = None
                    for (low, high), (f_low, f_high) in zip(pairs, faces[i]):
                        part = f_low * (v - low) + f_high * (v - high)
                        total = part if total is None else total + part
                    term = (0.5 * BETA) * total
                    reg_ref[c, z, at, pl.ds(i * LANES, LANES)] = term
                    acc = acc + v * term
        return acc

    acc = lax.fori_loop(0, sections, plane, jnp.zeros((TILE, LANES), jnp.float32))
    sum_ref[...] = acc
    out.wait()


def after(value, *gates):
    def kernel(*refs):
        del refs

    return pl.pallas_call(
        kernel,
        out_shape=jax.ShapeDtypeStruct(value.shape, value.dtype),
        in_specs=[ANY] * (1 + len(gates)),
        out_specs=ANY,
        input_output_aliases={0: 0},
    )(value, *gates)


def to_blocks(scan, extra, gate):
    count = lax.axis_size("row")
    sections, width, rows = scan.shape
    own = rows // count
    tall = own + 2 * extra
    if width == LANES and rows % width == 0:
        return call(
            block_kernel, [(count, sections, tall, width)], [VMEM, ANY], [(rows + 2 * TILE, width)]
        )(scan, gate)[0]
    turned = jnp.pad(jnp.swapaxes(scan, 1, 2), ((0, 0), (extra, extra), (0, 0)))
    return jnp.stack([turned[:, j * own : j * own + tall] for j in range(count)])


def to_rows(parts):
    parts = lax.all_to_all(parts, "row", split_axis=0, concat_axis=0, tiled=True)
    count, sections, own, width = parts.shape
    if width == LANES:
        return parts
    whole = parts.transpose(1, 2, 0, 3).reshape(sections, own, count * width // LANES, LANES)
    return whole.transpose(2, 0, 1, 3)


def summed(part, axis, lows):
    count = lax.axis_size(axis)
    got = [lax.ppermute(part, axis, [(i, i ^ low) for i in range(count)]) for low in lows]
    if len(got) == 3:
        place = lax.axis_index(axis) // lows[0] % 4
        pairs = (part + got[0], got[1] + got[2])
        return jnp.where(place < 2, pairs[0], pairs[1]) + jnp.where(place < 2, pairs[1], pairs[0])
    return part + got[0]


def stages(axis):
    count, near, found = lax.axis_size(axis), 1, []
    while near < count:
        if count % (4 * near) == 0:
            found.append((axis, (near, 2 * near, 3 * near)))
            near *= 4
        else:
            found.append((axis, (near,)))
            near *= 2
    return found


def call(kernel, shapes, ins, scratch=(), outs=None, flops=0):
    return pl.pallas_call(
        kernel,
        out_shape=[jax.ShapeDtypeStruct(shape, jnp.float32) for shape in shapes],
        in_specs=ins,
        out_specs=outs or [VMEM] * len(shapes),
        scratch_shapes=[
            pltpu.VMEM(shape, jnp.float32) if isinstance(shape, tuple) else pltpu.SemaphoreType.DMA((shape,))
            for shape in scratch
        ],
        compiler_params=pltpu.CompilerParams(vmem_limit_bytes=63 << 20),
        cost_estimate=pl.CostEstimate(flops=flops, bytes_accessed=4 << 20, transcendentals=0),
    )


def local(template_scan, reference_scan, velocity, stiffness):
    _, sections, rows, width = velocity.shape
    blocks = width // LANES
    tall, deep = rows + 2 * GAP, sections + 2 * WIDE
    own = (blocks, sections, rows, LANES)
    ends = (blocks, sections, SENT, LANES)
    sec, row = lax.axis_index("sec"), lax.axis_index("row")
    flags = jnp.stack([
        sec > 0, sec < lax.axis_size("sec") - 1, row > 0, row < lax.axis_size("row") - 1
    ]).astype(jnp.float32)

    lines = (3 * WIDE + 1) * sections
    low_rows, high_rows, low, high = call(
        pack_kernel,
        [(lines, width)] * 2 + [(3 * WIDE + 1, rows, width)] * 2,
        [VMEM] * 2,
        [8],
        [VMEM] * 2 + [ANY] * 2,
    )(velocity, stiffness)
    before, after_ = exchange(low_rows, high_rows, "row")
    template_blocks = to_blocks(template_scan, SENT, low_rows)
    template = to_rows(template_blocks)
    below, above = exchange(low, high, "sec")
    corners = call(corner_kernel, [(6 * WIDE * WIDE, width)] * 2, [VMEM] * 2)(before, after_)
    extended, reg, reg_sums = call(
        extend_kernel,
        [(3, blocks, deep, tall, LANES), velocity.shape, (TILE, LANES)],
        [VMEM] * 8,
        [(3, blocks, deep, tall, LANES), (blocks, sections + 2, tall, LANES), 1],
        [ANY, VMEM, VMEM],
        20 << 20,
    )(velocity, stiffness, below, above, before, after_, *exchange(*corners, "sec"))

    fixed_blocks = to_blocks(reference_scan, 0, template_blocks)
    low, high = call(slice_kernel, [(blocks, STEPS, tall, LANES)] * 2, [VMEM, ANY, ANY, ANY])(
        template, below, above, corners[0]
    )
    start = (template,) + exchange(low, high, "sec")
    fixed = to_rows(after(fixed_blocks, low))
    level = (blocks, sections + 2 * STEPS, tall, LANES)
    moved, kept = call(
        forward_kernel,
        [own, (STEPS - 1, blocks, sections + 2, tall, LANES)],
        [SMEM] + [ANY] * 4,
        [level] * STEPS + [(3, blocks, deep, tall, LANES), 3, deep, STEPS - 1],
        [VMEM, ANY],
        20 << 20,
    )(flags, *start, extended)

    misfit, low_rows, high_rows, partial = call(misfit_kernel, [own, ends, ends, (TILE, LANES)], [VMEM] * 3)(
        moved, fixed, reg_sums
    )
    before, after_ = exchange(low_rows, high_rows, "row")
    low, high = call(plane_kernel, [(blocks, WIDE, tall, LANES)] * 2, [VMEM] * 3)(misfit, before, after_)
    below, above = exchange(low, high, "sec")
    along = stages("row")
    partial = after(summed(partial, *along[0]), low)
    for stage in along[1:]:
        partial = summed(partial, *stage)
    partial = after(partial, below, above)
    (gradient,) = call(
        adjoint_kernel,
        [velocity.shape],
        [SMEM] + [VMEM] * 5 + [ANY] * 7,
        [(blocks, deep, tall, LANES)] * STEPS
        + [(3, blocks, deep, tall, LANES), (STEPS, blocks, sections + 2, tall, LANES)]
        + [velocity.shape] * 2 + [deep, STEPS + 2, 1, sections],
        [ANY],
        20 << 20,
    )(flags, misfit, below, above, before, after_, extended, *start, kept, reg, partial)
    for stage in stages("sec"):
        partial = summed(partial, *stage)

    voxels = sections * rows * width * lax.axis_size("sec") * lax.axis_size("row")
    objective = jnp.sum(partial) / voxels
    return (gradient, objective)


def solution(mesh):
    return jax.shard_map(
        local,
        mesh=mesh,
        in_specs=(
            P("sec", "row", None),
            P("sec", "row", None),
            P(None, "sec", "row", None),
            P("sec", "row", None),
        ),
        out_specs=(P(None, "sec", "row", None), P()),
        check_vma=False,
    )
```
